512 devices in a mesh: gx: 64 (over z, y), gy: 8 (over x, core).
Axes of the slice: x: 4, y: 4, z: 16, core: 2. Of those that a mesh axis runs over, the one named last changes fastest.
Arguments:
- density: float32 [512, 192, 2048], P('gx', 'gy'), may hold values from 0.1 to 4
- centers: float32 [8], replicated, may hold values from 0.3 to 3.5
- widths: float32 [8], replicated, may hold values from 0.3 to 1.2
- weights: float32 [8], replicated, may hold values from 0.1 to 1
- colors: float32 [3, 8], replicated, may hold values from 0.2 to 2
- light: float32 [3], replicated, may hold values from -3 to 3
Outputs:
- image: float32 [4, 192, 2048], P(None, 'gy', 'gx')
The draws below stay inside these ranges and needn't reach their ends.
All inputs are finite; a program needn't handle non-finite values.
Results may differ from the reference program's by a relative error of at most 0.00002.
Values sent between devices are 32-bit elements; how exact they have to be, the bound alone decides.
A program may use at most 64 MiB of HBM per device.

```python
import math
import jax
import jax.numpy as jnp
from jax import lax

SZ = 2048
K = 8
NX = 512
NY = 192


def level_of(rng, dims, pieces, smallest, largest):
    loudness = 1.0
    for axis_at, shards_of in pieces:
        steps = jax.random.uniform(jax.random.fold_in(jax.random.fold_in(rng, 6), axis_at), (shards_of,), jnp.float32, smallest / len(pieces), largest / len(pieces))
        loudness = loudness * jnp.repeat(jnp.exp(steps), dims[axis_at] // shards_of).reshape((-1,) + (1,) * (len(dims) - 1 - axis_at))
    return loudness


def normal_values(key, dims, scale, bound, kind=jnp.bfloat16):
    entries = jax.random.normal(key, dims, jnp.float32) * scale
    return jnp.minimum(jnp.maximum(entries, -bound), bound).astype(kind)


def setup_inputs(seed: int = 0) -> dict:
    arg_keys = jax.random.split(jax.random.key(seed), 7)
    return {
        "density": jnp.clip(jnp.exp(math.log(4.0) - 3.6888794 * jax.random.uniform(arg_keys[0], (NX, NY, SZ), jnp.float32) ** level_of(arg_keys[0], (NX, NY, SZ), ((0, 64), (1, 8)), -0.2, 0.2)), 0.1, 4.0),
        "centers": jnp.clip(jax.random.uniform(arg_keys[1], (K,), jnp.float32, 0.3, 3.5), 0.3, 3.5),
        "widths": jnp.clip(jnp.exp(jax.random.uniform(arg_keys[2], (K,), jnp.float32, math.log(0.3), math.log(1.2))), 0.3, 1.2),
        "weights": jnp.clip(jnp.exp(jax.random.uniform(arg_keys[3], (K,), jnp.float32, math.log(0.1), math.log(1.0))), 0.1, 1.0),
        "colors": jnp.clip(jax.random.uniform(arg_keys[4], (3, K), jnp.float32, 0.2, 2.0), 0.2, 2.0),
        "light": normal_values(arg_keys[5], (3,), 1.0, 3.0, jnp.float32),
    }


def sources(cells, grad_x, grad_y, grad_z, centers, widths, weights, colors, light):
    facing = light[0] * grad_x + light[1] * grad_y + light[2] * grad_z
    shading = 0.25 + 0.75 * jax.nn.sigmoid(2.0 * facing)
    extinction = jnp.zeros_like(cells)
    emitted = [jnp.zeros_like(cells) for channel in range(3)]
    for bump_index in range(centers.shape[0]):
        scaled = (cells - centers[bump_index]) / widths[bump_index]
        bump_value = jnp.exp(-scaled * scaled)
        extinction = extinction + weights[bump_index] * bump_value
        emitted = [emitted[channel] + colors[channel, bump_index] * bump_value for channel in range(3)]
    return extinction, [shading * source for source in emitted]


def march(cells, grad_x, grad_y, grad_z, centers, widths, weights, colors, light, step_size):
    extinction, emitted = sources(cells, grad_x, grad_y, grad_z, centers, widths, weights, colors, light)
    optical_step = step_size * extinction
    opacity = -jnp.expm1(-optical_step)
    before = jnp.cumsum(optical_step, axis=0) - optical_step
    weight = jnp.exp(-before) * opacity
    colour = jnp.stack([jnp.sum(weight * source, axis=0) for source in emitted])
    return colour, jnp.sum(optical_step, axis=0)


def reference(density, centers, widths, weights, colors, light):
    step_size = 1.5 / NX
    padded = jnp.pad(density, 1)

    def one_row(row_index):
        window = lax.dynamic_slice_in_dim(padded, row_index, 3, 1)
        cells = window[1:-1, 1, 1:-1]
        grad_x = 0.5 * (window[2:, 1, 1:-1] - window[:-2, 1, 1:-1])
        grad_y = 0.5 * (window[1:-1, 2, 1:-1] - window[1:-1, 0, 1:-1])
        grad_z = 0.5 * (window[1:-1, 1, 2:] - window[1:-1, 1, :-2])
        colour, optical = march(cells, grad_x, grad_y, grad_z, centers, widths, weights, colors, light, step_size)
        return jnp.concatenate([colour, (-jnp.expm1(-optical))[None]], 0)

    rows = lax.map(one_row, jnp.arange(NY, dtype=jnp.int32))
    return jnp.transpose(rows, (1, 0, 2))
```

```python
import functools
import math

import jax
import jax.numpy as jnp
from jax import lax
from jax.experimental import pallas as pl
from jax.experimental.pallas import tpu as pltpu
from jax.sharding import PartitionSpec as P

MESH = pl.DeviceIdType.MESH
LANES = 128
Q = 4
G = LANES // Q
PARTS = 4
SUB = 256


def roll_lanes(v, by):
    return pltpu.roll(v, by % LANES, axis=1)


def shifted(tiles, by, edge, lane_or_row, axis):
    size = tiles[0].shape[axis]
    rolled = [pltpu.roll(t, by % size, axis=axis) for t in tiles]
    if by > 0:
        before = [edge] + rolled[:-1]
        return [jnp.where(lane_or_row == 0, b, r) for b, r in zip(before, rolled)]
    after = rolled[1:] + [edge]
    return [jnp.where(lane_or_row == size - 1, a, r) for a, r in zip(after, rolled)]


def regroup(values, lane):
    a, b, c, d = values
    low = lane < 2 * G
    ac0 = jnp.where(low, a, roll_lanes(c, 2 * G))
    ac1 = jnp.where(low, roll_lanes(a, -2 * G), c)
    bd0 = jnp.where(low, b, roll_lanes(d, 2 * G))
    bd1 = jnp.where(low, roll_lanes(b, -2 * G), d)
    even = lax.rem(lane // G, 2) == 0
    out = []
    for first, second in ((ac0, bd0), (ac1, bd1)):
        out.append(jnp.where(even, first, roll_lanes(second, G)))
        out.append(jnp.where(even, roll_lanes(first, -G), second))
    return out


def over(front, back, lane):
    clear = 1.0 - front
    ends = jnp.where(lane < G, roll_lanes(clear, G), clear)
    inner = (lane >= G) & (lane < 3 * G)
    return front + jnp.where(inner, roll_lanes(ends, 2 * G), ends) * back


def kernel(
    nx, ny, step_size, density, centers, widths, weights, colors, light, out,
    x, rows_out, rows_in, depth_in, prm, emi, p1s, p1r, p2s, p2r,
    x_sem, rows_ss, rows_rs, depth_ss, depth_rs, p1_ss, p1_rs, p2_ss, p2_rs,
):
    layers, rows, cols = density.shape
    nz = nx // Q
    bumps = centers.shape[0]
    width = cols // PARTS
    per = width // LANES
    me, my = lax.axis_index("gx"), lax.axis_index("gy")
    z, y = me // Q, lax.rem(me, Q)
    nxt, prv = lax.rem(me + 1, nx), lax.rem(me + nx - 1, nx)
    down, up = lax.rem(my + 1, ny), lax.rem(my + ny - 1, ny)

    load = pltpu.make_async_copy(density, x.at[:, :, pl.ds(LANES, cols)], x_sem)
    load.start()

    barrier = pltpu.get_barrier_semaphore()

    def greet(gx, gy):
        pl.semaphore_signal(barrier, inc=1, device_id=(gx, gy), device_id_type=MESH)

    greet(nxt, my)
    greet(prv, my)
    greet(me, down)
    greet(me, up)

    def greet_y(k, _):
        greet(z * Q + lax.rem(y + k, Q), my)
        return 0

    def greet_z(k, _):
        greet(lax.rem(z + k, nz) * Q + y, my)
        return 0

    lax.fori_loop(1, Q, greet_y, 0)
    lax.fori_loop(1, nz, greet_z, 0)

    tile = (8, LANES)
    scale = math.sqrt(math.log2(math.e))
    for k in range(bumps):
        weight = jnp.full(tile, weights[k] * step_size, jnp.float32)
        prm[6 * k] = jnp.full(tile, centers[k], jnp.float32)
        prm[6 * k + 1] = scale / jnp.full(tile, widths[k], jnp.float32)
        prm[6 * k + 2] = jnp.log2(weight)
        for c in range(3):
            prm[6 * k + 3 + c] = jnp.full(tile, colors[c, k], jnp.float32) / weight
    for c in range(3):
        prm[6 * bumps + c] = jnp.full(tile, 0.5 * light[c], jnp.float32)
    x[:, :, :LANES] = jnp.zeros((layers, rows, LANES), jnp.float32)
    x[:, :, LANES + cols :] = jnp.zeros((layers, rows, LANES), jnp.float32)

    load.wait()
    for l in range(layers):
        rows_out[0, l : l + 1, :] = x[l, 0:1, LANES : LANES + cols]
        rows_out[1, l : l + 1, :] = x[l, rows - 1 : rows, LANES : LANES + cols]

    def part_at(s, place):
        return lax.rem(place // Q + jnp.where(s == 0, 2, jnp.where(s == 1, 1, jnp.where(s == 2, 3, 0))), PARTS)

    def rows_copy(side, s):
        at = pl.ds(pl.multiple_of(part_at(s, z) * width, width), width)
        return pltpu.make_async_remote_copy(
            src_ref=rows_out.at[1 - side, :, at],
            dst_ref=rows_in.at[side, :, at],
            send_sem=rows_ss.at[side, s],
            recv_sem=rows_rs.at[side, s],
            device_id=(me, down if side == 0 else up),
            device_id_type=MESH,
        )

    def depth_copy(side, s, place, gx):
        start = pl.multiple_of(part_at(s, place) * width, width)
        return pltpu.make_async_remote_copy(
            src_ref=x.at[layers - 1 if side == 0 else 0, :, pl.ds(pl.multiple_of(start + LANES, LANES), width)],
            dst_ref=depth_in.at[side, :, pl.ds(start, width)],
            send_sem=depth_ss.at[side, s],
            recv_sem=depth_rs.at[side, s],
            device_id=(gx, my),
            device_id_type=MESH,
        )

    def p1_copy(s, k):
        to = lax.rem(y + k, Q)
        return pltpu.make_async_remote_copy(
            src_ref=p1s.at[s, to],
            dst_ref=p1r.at[s, k],
            send_sem=p1_ss.at[s, k],
            recv_sem=p1_rs.at[s, k],
            device_id=(z * Q + to, my),
            device_id_type=MESH,
        )

    def p2_copy(to):
        k = lax.rem(to + nz - z, nz)
        return pltpu.make_async_remote_copy(
            src_ref=p2s.at[to],
            dst_ref=p2r.at[k],
            send_sem=p2_ss.at[k],
            recv_sem=p2_rs.at[k],
            device_id=(to * Q + y, my),
            device_id_type=MESH,
        )

    pl.semaphore_wait(barrier, 4 + (Q - 1) + (nz - 1))

    def send_halos(s, _):
        for side in range(2):
            rows_copy(side, s).start()
        depth_copy(0, s, nxt // Q, nxt).start()
        depth_copy(1, s, prv // Q, prv).start()
        return 0

    lax.fori_loop(0, PARTS, send_halos, 0)

    lane = lax.broadcasted_iota(jnp.int32, tile, 1)
    row = lax.broadcasted_iota(jnp.int32, tile, 0)
    lane_all = lax.broadcasted_iota(jnp.int32, (rows, LANES), 1)
    lane_part = lax.broadcasted_iota(jnp.int32, (per, rows, LANES), 2)
    from_prv = jnp.where(me > 0, 1.0, 0.0).astype(jnp.float32)
    from_nxt = jnp.where(me < nx - 1, 1.0, 0.0).astype(jnp.float32)
    from_up = jnp.where(my > 0, 1.0, 0.0).astype(jnp.float32)
    from_down = jnp.where(my < ny - 1, 1.0, 0.0).astype(jnp.float32)
    reps = (rows // 8, SUB // LANES)

    def wide(i):
        return jnp.tile(prm[i], reps)

    def emit(part):
        def one(i, _):
            l, start = lax.rem(i, layers), (i // layers) * SUB
            cells = x[l, :, pl.ds(pl.multiple_of(part * width + start + LANES, LANES), SUB)]
            sums = None
            for k in range(bumps):
                scaled = (cells - wide(6 * k)) * wide(6 * k + 1)
                step = jnp.exp2(wide(6 * k + 2) - scaled * scaled)
                terms = [step] + [step * wide(6 * k + 3 + c) for c in range(3)]
                sums = terms if sums is None else [a + b for a, b in zip(sums, terms)]
            t = sums[0]
            opacity = t * (1.0 - t * (0.5 - t * (1.0 / 6.0 - t * (1.0 / 24.0))))
            at = pl.ds(pl.multiple_of(start, SUB), SUB)
            for c, v in enumerate([opacity] + sums[1:]):
                emi[c, l, :, at] = v
            return 0

        lax.fori_loop(0, layers * (width // SUB), one, 0)

    n_lane, n_row = SUB // LANES, rows // 8

    def grid_of(v):
        return [[v[8 * r : 8 * r + 8, LANES * c : LANES * c + LANES] for c in range(v.shape[1] // LANES)] for r in range(v.shape[0] // 8)]

    def joined(tiles):
        return jnp.concatenate([jnp.concatenate(line, 1) for line in tiles], 0)

    def march(s, part):
        def one(i, _):
            at = pl.multiple_of(part * width + i * SUB, SUB)
            here = pl.ds(pl.multiple_of(i * SUB, SUB), SUB)
            hx, hy, hz = (wide(6 * bumps + c) for c in range(3))
            clear = jnp.ones((rows, SUB), jnp.float32)
            opaque = jnp.zeros((rows, SUB), jnp.float32)
            colour = [jnp.zeros((rows, SUB), jnp.float32) for c in range(3)]

            def layer(l):
                return x[l, :, pl.ds(pl.multiple_of(at + LANES, LANES), SUB)]

            before, cells = depth_in[0, :, pl.ds(at, SUB)] * from_prv, layer(0)
            for l in range(layers):
                after = layer(l + 1) if l < layers - 1 else depth_in[1, :, pl.ds(at, SUB)] * from_nxt
                tiles = grid_of(cells)
                left = grid_of(x[l, :, pl.ds(at, LANES)])
                right = grid_of(x[l, :, pl.ds(pl.multiple_of(at + LANES + SUB, LANES), LANES)])
                behind = [shifted(tiles[r], 1, roll_lanes(left[r][0], 1), lane, 1) for r in range(n_row)]
                ahead = [shifted(tiles[r], -1, roll_lanes(right[r][0], -1), lane, 1) for r in range(n_row)]
                over_row = jnp.broadcast_to(rows_in[0, l : l + 1, pl.ds(at, SUB)], (8, SUB)) * from_up
                under_row = jnp.broadcast_to(rows_in[1, l : l + 1, pl.ds(at, SUB)], (8, SUB)) * from_down
                above, below = [], []
                for c in range(n_lane):
                    column = [tiles[r][c] for r in range(n_row)]
                    above.append(shifted(column, 1, over_row[:, LANES * c : LANES * c + LANES], row, 0))
                    below.append(shifted(column, -1, under_row[:, LANES * c : LANES * c + LANES], row, 0))
                above = [[above[c][r] for c in range(n_lane)] for r in range(n_row)]
                below = [[below[c][r] for c in range(n_lane)] for r in range(n_row)]
                facing = (
                    hx * (after - before)
                    + hy * (joined(below) - joined(above))
                    + hz * (joined(ahead) - joined(behind))
                )
                shading = 0.625 + 0.375 * jnp.tanh(facing)
                seen = clear * emi[0, l, :, here]
                clear, opaque = clear - seen, opaque + seen
                lit = seen * shading
                colour = [colour[c] + lit * emi[c + 1, l, :, here] for c in range(3)]
                before, cells = cells, after
            for b in range(n_lane):
                cut = slice(LANES * b, LANES * b + LANES)
                owned = regroup([v[:, cut] for v in colour + [opaque]], lane_all)
                for j in range(Q):
                    p1s[s, j, i * n_lane + b] = owned[j]
            return 0

        lax.fori_loop(0, width // SUB, one, 0)

    def step(s, _):
        @pl.when(s < PARTS)
        def _():
            part = part_at(s, z)
            emit(part)
            for side in range(2):
                rows_copy(side, s).wait_recv()
                depth_copy(side, s, z, (nxt, prv)[side]).wait_recv()
            march(s, part)
            for k in (2, 1, 3):
                p1_copy(s, k).start()

        @pl.when(s > 0)
        def _():
            t = s - 1
            part = part_at(t, z)
            p1r[t, 0] = p1s[t, y]
            for k in range(1, Q):
                p1_copy(t, k).wait_recv()
            total = p1r[t, lax.rem(y + 1, Q)]
            for j in range(Q - 2, -1, -1):
                total = over(p1r[t, lax.rem(y + Q - j, Q)].reshape(per * rows, LANES), total.reshape(per * rows, LANES), lane_flat)
            total = total.reshape(per, rows, LANES)
            for b in range(per):
                to = part * per + b
                p2s[to] = total[b]

                @pl.when(to != z)
                def _():
                    p2_copy(to).start()

        return 0

    lane_flat = lax.broadcasted_iota(jnp.int32, (per * rows, LANES), 1)
    lax.fori_loop(0, PARTS + 1, step, 0)

    p2r[0] = p2s[z]

    def wait_p2(k, _):
        p2_copy(lax.rem(z + k, nz)).wait_recv()
        return 0

    lax.fori_loop(1, nz, wait_p2, 0)

    def behind_all(i, total):
        return over(p2r[lax.rem(z + 1 + i, nz)], total, lane_all)

    total = lax.fori_loop(1, nz, behind_all, p2r[lax.rem(z + 1, nz)])
    for c in range(4):
        out[c] = total[:, G * c : G * c + G]

    def finish_halos(s, _):
        for side in range(2):
            rows_copy(side, s).wait_send()
            depth_copy(side, s, z, (nxt, prv)[side]).wait_send()
        for k in range(1, Q):
            p1_copy(s, k).wait_send()
        return 0

    lax.fori_loop(0, PARTS, finish_halos, 0)

    def finish_p2(k, _):
        p2_copy(lax.rem(z + k, nz)).wait_send()
        return 0

    lax.fori_loop(1, nz, finish_p2, 0)


def local(nx, ny, density, centers, widths, weights, colors, light):
    layers, rows, cols = density.shape
    nz, bumps = nx // Q, centers.shape[0]
    width = cols // PARTS
    per = width // LANES
    dma = pltpu.SemaphoreType.DMA
    smem = pl.BlockSpec(memory_space=pltpu.SMEM)
    f32 = jnp.float32
    return pl.pallas_call(
        functools.partial(kernel, nx, ny, 1.5 / (layers * nx)),
        out_shape=jax.ShapeDtypeStruct((4, rows, cols // nx), f32),
        in_specs=[pl.BlockSpec(memory_space=pl.ANY)] + [smem] * 5,
        out_specs=pl.BlockSpec(memory_space=pltpu.VMEM),
        scratch_shapes=[
            pltpu.VMEM((layers, rows, cols + 2 * LANES), f32),
            pltpu.VMEM((2, layers, cols), f32),
            pltpu.VMEM((2, layers, cols), f32),
            pltpu.VMEM((2, rows, cols), f32),
            pltpu.VMEM((6 * bumps + 3, 8, LANES), f32),
            pltpu.VMEM((4, layers, rows, width), f32),
            pltpu.VMEM((PARTS, Q, per, rows, LANES), f32),
            pltpu.VMEM((PARTS, Q, per, rows, LANES), f32),
            pltpu.VMEM((nz, rows, LANES), f32),
            pltpu.VMEM((nz, rows, LANES), f32),
            dma,
            dma((2, PARTS)),
            dma((2, PARTS)),
            dma((2, PARTS)),
            dma((2, PARTS)),
            dma((PARTS, Q)),
            dma((PARTS, Q)),
            dma((nz,)),
            dma((nz,)),
        ],
        compiler_params=pltpu.CompilerParams(
            collective_id=0, has_side_effects=True, vmem_limit_bytes=40 * 1024 * 1024
        ),
        cost_estimate=pl.CostEstimate(
            flops=130 * density.size, bytes_accessed=4 * density.size, transcendentals=9 * density.size
        ),
    )(density, centers, widths, weights, colors, light)


def solution(mesh):
    nx, ny = mesh.shape["gx"], mesh.shape["gy"]
    in_specs = (P("gx", "gy", None), P(), P(), P(), P(), P())
    out_specs = P(None, "gy", "gx")
    return jax.shard_map(
        functools.partial(local, nx, ny), mesh=mesh, in_specs=in_specs, out_specs=out_specs, check_vma=False
    )
```

```python
import functools
import math

import jax
import jax.numpy as jnp
from jax import lax
from jax.experimental import pallas as pl
from jax.experimental.pallas import tpu as pltpu
from jax.sharding import PartitionSpec as P

MESH = pl.DeviceIdType.MESH
LANES = 128
Q = 4
G = LANES // Q
PARTS = 8
SUB = 256


def roll_lanes(v, by):
    return pltpu.roll(v, by % LANES, axis=1)


def shifted(tiles, by, edge, lane_or_row, axis):
    size = tiles[0].shape[axis]
    rolled = [pltpu.roll(t, by % size, axis=axis) for t in tiles]
    if by > 0:
        before = [edge] + rolled[:-1]
        return [jnp.where(lane_or_row == 0, b, r) for b, r in zip(before, rolled)]
    after = rolled[1:] + [edge]
    return [jnp.where(lane_or_row == size - 1, a, r) for a, r in zip(after, rolled)]


def regroup(values, lane):
    a, b, c, d = values
    low = lane < 2 * G
    ac0 = jnp.where(low, a, roll_lanes(c, 2 * G))
    ac1 = jnp.where(low, roll_lanes(a, -2 * G), c)
    bd0 = jnp.where(low, b, roll_lanes(d, 2 * G))
    bd1 = jnp.where(low, roll_lanes(b, -2 * G), d)
    even = lax.rem(lane // G, 2) == 0
    out = []
    for first, second in ((ac0, bd0), (ac1, bd1)):
        out.append(jnp.where(even, first, roll_lanes(second, G)))
        out.append(jnp.where(even, roll_lanes(first, -G), second))
    return out


def over(front, back, lane):
    clear = 1.0 - front
    ends = jnp.where(lane < G, roll_lanes(clear, G), clear)
    inner = (lane >= G) & (lane < 3 * G)
    return front + jnp.where(inner, roll_lanes(ends, 2 * G), ends) * back


def kernel(
    nx, ny, step_size, density, *rest,
):
    given, rest = rest[:5], rest[5:]
    out, centers, widths, weights, colors, light = rest[:6]
    x, rows_out, rows_in, depth_in, prm, emi, p1s, p1r, pair, r1r, p2s, p2r = rest[6:18]
    x_sem, given_sem, rows_ss, rows_rs, depth_ss, depth_rs, p1_ss, p1_rs, r1_ss, r1_rs, p2_ss, p2_rs = rest[18:]
    layers, rows, cols = density.shape
    nz = nx // Q
    bumps = centers.shape[0]
    width = cols // PARTS
    per = width // LANES
    me, my = lax.axis_index("gx"), lax.axis_index("gy")
    z, y = me // Q, lax.rem(me, Q)
    partner, mirror = y + 1 - 2 * lax.rem(y, 2), Q - 1 - y
    kept = jnp.where((y == 0) | (y == Q - 1), 0, 2)
    own = y // 2
    nxt, prv = lax.rem(me + 1, nx), lax.rem(me + nx - 1, nx)
    down, up = lax.rem(my + 1, ny), lax.rem(my + ny - 1, ny)

    load = pltpu.make_async_copy(density, x.at[:, :, pl.ds(LANES, cols)], x_sem)
    load.start()
    fetches = [
        pltpu.make_async_copy(src, dst, given_sem.at[i])
        for i, (src, dst) in enumerate(zip(given, (centers, widths, weights, colors, light)))
    ]
    for fetch in fetches:
        fetch.start()

    barrier = pltpu.get_barrier_semaphore()

    def greet(gx, gy):
        pl.semaphore_signal(barrier, inc=1, device_id=(gx, gy), device_id_type=MESH)

    greet(nxt, my)
    greet(prv, my)
    greet(me, down)
    greet(me, up)

    def greet_z(k, _):
        greet(lax.rem(z + k, nz) * Q + y, my)
        return 0

    greet(z * Q + partner, my)
    greet(z * Q + mirror, my)
    lax.fori_loop(1, nz, greet_z, 0)
    x[:, :, :LANES] = jnp.zeros((layers, rows, LANES), jnp.float32)
    x[:, :, LANES + cols :] = jnp.zeros((layers, rows, LANES), jnp.float32)

    def part_at(s, place):
        away = jnp.where(lax.rem(s, 2) == 0, s // 2, PARTS - (s + 1) // 2)
        return lax.rem(place // per + PARTS // 2 + away, PARTS)

    def rows_copy(side):
        return pltpu.make_async_remote_copy(
            src_ref=rows_out.at[1 - side],
            dst_ref=rows_in.at[side],
            send_sem=rows_ss.at[side],
            recv_sem=rows_rs.at[side],
            device_id=(me, down if side == 0 else up),
            device_id_type=MESH,
        )

    def depth_copy(side, s, place, gx):
        start = pl.multiple_of(part_at(s, place) * width, width)
        return pltpu.make_async_remote_copy(
            src_ref=density.at[layers - 1 if side == 0 else 0, :, pl.ds(start, width)],
            dst_ref=depth_in.at[side, :, pl.ds(start, width)],
            send_sem=depth_ss.at[side, s],
            recv_sem=depth_rs.at[side, s],
            device_id=(gx, my),
            device_id_type=MESH,
        )

    def p1_copy(s):
        return pltpu.make_async_remote_copy(
            src_ref=p1s.at[s, pl.ds(2 - kept, 2)],
            dst_ref=p1r.at[s],
            send_sem=p1_ss.at[s],
            recv_sem=p1_rs.at[s],
            device_id=(z * Q + partner, my),
            device_id_type=MESH,
        )

    def r1_copy(s):
        return pltpu.make_async_remote_copy(
            src_ref=pair.at[s, 1 - own],
            dst_ref=r1r.at[s],
            send_sem=r1_ss.at[s],
            recv_sem=r1_rs.at[s],
            device_id=(z * Q + mirror, my),
            device_id_type=MESH,
        )

    def p2_copy(to):
        k = lax.rem(to + nz - z, nz)
        return pltpu.make_async_remote_copy(
            src_ref=p2s.at[to],
            dst_ref=p2r.at[k],
            send_sem=p2_ss.at[k],
            recv_sem=p2_rs.at[k],
            device_id=(to * Q + y, my),
            device_id_type=MESH,
        )

    for fetch in fetches:
        fetch.wait()
    tile = (8, LANES)
    scale = math.sqrt(math.log2(math.e))
    for k in range(bumps):
        weight = jnp.full(tile, weights[k] * step_size, jnp.float32)
        prm[6 * k] = jnp.full(tile, centers[k], jnp.float32)
        prm[6 * k + 1] = scale / jnp.full(tile, widths[k], jnp.float32)
        prm[6 * k + 2] = jnp.log2(weight)
        for c in range(3):
            prm[6 * k + 3 + c] = jnp.full(tile, colors[c, k], jnp.float32) / weight
    for c in range(3):
        prm[6 * bumps + c] = jnp.full(tile, 0.5 * light[c], jnp.float32)

    load.wait()
    for l in range(layers):
        rows_out[0, l : l + 1, :] = x[l, 0:1, LANES : LANES + cols]
        rows_out[1, l : l + 1, :] = x[l, rows - 1 : rows, LANES : LANES + cols]

    pl.semaphore_wait(barrier, 4 + 2 + (nz - 1))

    def send_depth(s):
        depth_copy(0, s, nxt // Q, nxt).start()
        depth_copy(1, s, prv // Q, prv).start()

    send_depth(0)
    for side in range(2):
        rows_copy(side).start()
    send_depth(1)

    lane = lax.broadcasted_iota(jnp.int32, tile, 1)
    row = lax.broadcasted_iota(jnp.int32, tile, 0)
    lane_all = lax.broadcasted_iota(jnp.int32, (rows, LANES), 1)
    from_prv = jnp.where(me > 0, 1.0, 0.0).astype(jnp.float32)
    from_nxt = jnp.where(me < nx - 1, 1.0, 0.0).astype(jnp.float32)
    from_up = jnp.where(my > 0, 1.0, 0.0).astype(jnp.float32)
    from_down = jnp.where(my < ny - 1, 1.0, 0.0).astype(jnp.float32)
    reps = (rows // 8, SUB // LANES)

    def wide(i):
        return jnp.tile(prm[i], reps)

    def emit(part):
        def one(i, _):
            l, start = lax.rem(i, layers), (i // layers) * SUB
            cells = x[l, :, pl.ds(pl.multiple_of(part * width + start + LANES, LANES), SUB)]
            sums = None
            for k in range(bumps):
                scaled = (cells - wide(6 * k)) * wide(6 * k + 1)
                step = jnp.exp2(wide(6 * k + 2) - scaled * scaled)
                terms = [step] + [step * wide(6 * k + 3 + c) for c in range(3)]
                sums = terms if sums is None else [a + b for a, b in zip(sums, terms)]
            t = sums[0]
            opacity = t * (1.0 - t * (0.5 - t * (1.0 / 6.0 - t * (1.0 / 24.0))))
            at = pl.ds(pl.multiple_of(start, SUB), SUB)
            for c, v in enumerate([opacity] + sums[1:]):
                emi[c, l, :, at] = v
            return 0

        lax.fori_loop(0, layers * (width // SUB), one, 0)

    n_lane, n_row = SUB // LANES, rows // 8

    def grid_of(v):
        return [[v[8 * r : 8 * r + 8, LANES * c : LANES * c + LANES] for c in range(v.shape[1] // LANES)] for r in range(v.shape[0] // 8)]

    def joined(tiles):
        return jnp.concatenate([jnp.concatenate(line, 1) for line in tiles], 0)

    def march(s, part):
        def one(i, _):
            at = pl.multiple_of(part * width + i * SUB, SUB)
            here = pl.ds(pl.multiple_of(i * SUB, SUB), SUB)
            hx, hy, hz = (wide(6 * bumps + c) for c in range(3))
            clear = jnp.ones((rows, SUB), jnp.float32)
            opaque = jnp.zeros((rows, SUB), jnp.float32)
            colour = [jnp.zeros((rows, SUB), jnp.float32) for c in range(3)]

            def layer(l):
                return x[l, :, pl.ds(pl.multiple_of(at + LANES, LANES), SUB)]

            before, cells = depth_in[0, :, pl.ds(at, SUB)] * from_prv, layer(0)
            for l in range(layers):
                after = layer(l + 1) if l < layers - 1 else depth_in[1, :, pl.ds(at, SUB)] * from_nxt
                tiles = grid_of(cells)
                left = grid_of(x[l, :, pl.ds(at, LANES)])
                right = grid_of(x[l, :, pl.ds(pl.multiple_of(at + LANES + SUB, LANES), LANES)])
                behind = [shifted(tiles[r], 1, roll_lanes(left[r][0], 1), lane, 1) for r in range(n_row)]
                ahead = [shifted(tiles[r], -1, roll_lanes(right[r][0], -1), lane, 1) for r in range(n_row)]
                over_row = jnp.broadcast_to(rows_in[0, l : l + 1, pl.ds(at, SUB)], (8, SUB)) * from_up
                under_row = jnp.broadcast_to(rows_in[1, l : l + 1, pl.ds(at, SUB)], (8, SUB)) * from_down
                above, below = [], []
                for c in range(n_lane):
                    column = [tiles[r][c] for r in range(n_row)]
                    above.append(shifted(column, 1, over_row[:, LANES * c : LANES * c + LANES], row, 0))
                    below.append(shifted(column, -1, under_row[:, LANES * c : LANES * c + LANES], row, 0))
                above = [[above[c][r] for c in range(n_lane)] for r in range(n_row)]
                below = [[below[c][r] for c in range(n_lane)] for r in range(n_row)]
                facing = (
                    hx * (after - before)
                    + hy * (joined(below) - joined(above))
                    + hz * (joined(ahead) - joined(behind))
                )
                shading = 0.625 + 0.375 * jnp.tanh(facing)
                seen = clear * emi[0, l, :, here]
                clear, opaque = clear - seen, opaque + seen
                lit = seen * shading
                colour = [colour[c] + lit * emi[c + 1, l, :, here] for c in range(3)]
                before, cells = cells, after
            for b in range(n_lane):
                cut = slice(LANES * b, LANES * b + LANES)
                owned = regroup([v[:, cut] for v in colour + [opaque]], lane_all)
                for place, j in enumerate((0, 3, 1, 2)):
                    p1s[s, place, i * n_lane + b] = owned[j]
            return 0

        lax.fori_loop(0, width // SUB, one, 0)

    def ordered(mine, theirs, mine_first):
        return jnp.where(mine_first, mine, theirs), jnp.where(mine_first, theirs, mine)

    def step(s, _):
        @pl.when(s < PARTS)
        def _():
            part = part_at(s, z)

            @pl.when(s + 2 < PARTS)
            def _():
                send_depth(s + 2)

            emit(part)

            @pl.when(s == 0)
            def _():
                for side in range(2):
                    rows_copy(side).wait_recv()

            for side in range(2):
                depth_copy(side, s, z, (nxt, prv)[side]).wait_recv()
            march(s, part)
            p1_copy(s).start()

        @pl.when((s >= 2) & (s < PARTS + 2))
        def _():
            t = s - 2
            p1_copy(t).wait_recv()
            flat = (2 * per * rows, LANES)
            mine, theirs = p1s[t, pl.ds(kept, 2)].reshape(flat), p1r[t].reshape(flat)
            front, back = ordered(mine, theirs, partner > y)
            lane_flat = lax.broadcasted_iota(jnp.int32, flat, 1)
            pair[t] = over(front, back, lane_flat).reshape(2, per, rows, LANES)
            r1_copy(t).start()

        @pl.when(s >= 4)
        def _():
            t = s - 4
            part = part_at(t, z)
            r1_copy(t).wait_recv()
            flat = (per * rows, LANES)
            front, back = ordered(pair[t, own].reshape(flat), r1r[t].reshape(flat), mirror > y)
            lane_flat = lax.broadcasted_iota(jnp.int32, flat, 1)
            total = over(front, back, lane_flat).reshape(per, rows, LANES)
            for b in range(per):
                to = part * per + b
                p2s[to] = total[b]

                @pl.when(to != z)
                def _():
                    p2_copy(to).start()

        return 0

    lax.fori_loop(0, PARTS + 4, step, 0)

    p2r[0] = p2s[z]

    for side in range(2):
        rows_copy(side).wait_send()

    def finish(s, _):
        for side in range(2):
            depth_copy(side, s, z, (nxt, prv)[side]).wait_send()
        p1_copy(s).wait_send()
        r1_copy(s).wait_send()
        return 0

    lax.fori_loop(0, PARTS, finish, 0)

    def wait_p2(k, _):
        p2_copy(lax.rem(z + k, nz)).wait()
        return 0

    lax.fori_loop(1, nz, wait_p2, 0)

    total = p2r[lax.rem(z + 1, nz)]
    for i in range(1, nz):
        total = over(p2r[lax.rem(z + 1 + i, nz)], total, lane_all)
    for c in range(4):
        out[c] = total[:, G * c : G * c + G]


def local(nx, ny, density, centers, widths, weights, colors, light):
    layers, rows, cols = density.shape
    nz, bumps = nx // Q, centers.shape[0]
    width = cols // PARTS
    per = width // LANES
    dma = pltpu.SemaphoreType.DMA
    hbm = pl.BlockSpec(memory_space=pltpu.HBM)
    f32 = jnp.float32
    return pl.pallas_call(
        functools.partial(kernel, nx, ny, 1.5 / (layers * nx)),
        out_shape=jax.ShapeDtypeStruct((4, rows, cols // nx), f32),
        in_specs=[hbm] * 6,
        out_specs=pl.BlockSpec(memory_space=pltpu.VMEM),
        scratch_shapes=[pltpu.SMEM(given.shape, f32) for given in (centers, widths, weights, colors, light)]
        + [
            pltpu.VMEM((layers, rows, cols + 2 * LANES), f32),
            pltpu.VMEM((2, layers, cols), f32),
            pltpu.VMEM((2, layers, cols), f32),
            pltpu.VMEM((2, rows, cols), f32),
            pltpu.VMEM((6 * bumps + 3, 8, LANES), f32),
            pltpu.VMEM((4, layers, rows, width), f32),
            pltpu.VMEM((PARTS, Q, per, rows, LANES), f32),
            pltpu.VMEM((PARTS, 2, per, rows, LANES), f32),
            pltpu.VMEM((PARTS, 2, per, rows, LANES), f32),
            pltpu.VMEM((PARTS, per, rows, LANES), f32),
            pltpu.VMEM((nz, rows, LANES), f32),
            pltpu.VMEM((nz, rows, LANES), f32),
            dma,
            dma((5,)),
            dma((2,)),
            dma((2,)),
            dma((2, PARTS)),
            dma((2, PARTS)),
            dma((PARTS,)),
            dma((PARTS,)),
            dma((PARTS,)),
            dma((PARTS,)),
            dma((nz,)),
            dma((nz,)),
        ],
        compiler_params=pltpu.CompilerParams(
            collective_id=0, has_side_effects=True, vmem_limit_bytes=40 * 1024 * 1024
        ),
        cost_estimate=pl.CostEstimate(
            flops=130 * density.size, bytes_accessed=4 * density.size, transcendentals=9 * density.size
        ),
    )(*(pltpu.with_memory_space_constraint(v, pltpu.HBM) for v in (density, centers, widths, weights, colors, light)))


def solution(mesh):
    nx, ny = mesh.shape["gx"], mesh.shape["gy"]
    in_specs = (P("gx", "gy", None), P(), P(), P(), P(), P())
    out_specs = P(None, "gy", "gx")
    return jax.shard_map(
        functools.partial(local, nx, ny), mesh=mesh, in_specs=in_specs, out_specs=out_specs, check_vma=False
    )
```

```python
import functools
import math

import jax
import jax.numpy as jnp
from jax import lax
from jax.experimental import pallas as pl
from jax.experimental.pallas import tpu as pltpu
from jax.sharding import PartitionSpec as P

MESH = pl.DeviceIdType.MESH
LANES = 128
Q = 4
G = LANES // Q
PARTS = 8
LEAD = 3
SUB = 256


def roll_lanes(v, by):
    return pltpu.roll(v, by % LANES, axis=1)


def shifted(tiles, by, edge, lane_or_row, axis):
    size = tiles[0].shape[axis]
    rolled = [pltpu.roll(t, by % size, axis=axis) for t in tiles]
    if by > 0:
        before = [edge] + rolled[:-1]
        return [jnp.where(lane_or_row == 0, b, r) for b, r in zip(before, rolled)]
    after = rolled[1:] + [edge]
    return [jnp.where(lane_or_row == size - 1, a, r) for a, r in zip(after, rolled)]


def regroup(values, lane):
    a, b, c, d = values
    low = lane < 2 * G
    ac0 = jnp.where(low, a, roll_lanes(c, 2 * G))
    ac1 = jnp.where(low, roll_lanes(a, -2 * G), c)
    bd0 = jnp.where(low, b, roll_lanes(d, 2 * G))
    bd1 = jnp.where(low, roll_lanes(b, -2 * G), d)
    even = lax.rem(lane // G, 2) == 0
    out = []
    for first, second in ((ac0, bd0), (ac1, bd1)):
        out.append(jnp.where(even, first, roll_lanes(second, G)))
        out.append(jnp.where(even, roll_lanes(first, -G), second))
    return out


def over(front, back, lane):
    clear = 1.0 - front
    ends = jnp.where(lane < G, roll_lanes(clear, G), clear)
    inner = (lane >= G) & (lane < 3 * G)
    return front + jnp.where(inner, roll_lanes(ends, 2 * G), ends) * back


def kernel(
    nx, ny, step_size, density, *rest,
):
    given, rest = rest[:5], rest[5:]
    out, centers, widths, weights, colors, light = rest[:6]
    x, rows_out, rows_in, depth_in, prm, emi, p1s, p1r, lastr, p2s, p2r = rest[6:17]
    x_sem, given_sem, rows_ss, rows_rs, depth_ss, depth_rs, p1_ss, p1_rs, last_ss, last_rs, p2_ss, p2_rs = rest[17:]
    layers, rows, cols = density.shape
    nz = nx // Q
    bumps = centers.shape[0]
    width = cols // PARTS
    per = width // LANES
    me, my = lax.axis_index("gx"), lax.axis_index("gy")
    z, y = me // Q, lax.rem(me, Q)
    first_z, in_group = z // per * per, lax.rem(z, per)
    nxt, prv = lax.rem(me + 1, nx), lax.rem(me + nx - 1, nx)
    down, up = lax.rem(my + 1, ny), lax.rem(my + ny - 1, ny)

    load = pltpu.make_async_copy(density, x.at[:, :, pl.ds(LANES, cols)], x_sem)
    load.start()
    fetches = [
        pltpu.make_async_copy(src, dst, given_sem.at[i])
        for i, (src, dst) in enumerate(zip(given, (centers, widths, weights, colors, light)))
    ]
    for fetch in fetches:
        fetch.start()

    barrier = pltpu.get_barrier_semaphore()

    def greet(gx, gy):
        pl.semaphore_signal(barrier, inc=1, device_id=(gx, gy), device_id_type=MESH)

    greet(nxt, my)
    greet(prv, my)
    greet(me, down)
    greet(me, up)

    def greet_z(k, _):
        greet(lax.rem(z + k, nz) * Q + y, my)
        return 0

    lax.fori_loop(1, nz, greet_z, 0)
    for k in range(1, Q):
        for g in range(per):
            greet((first_z + lax.rem(in_group + g, per)) * Q + lax.rem(y + k, Q), my)
    x[:, :, :LANES] = jnp.zeros((layers, rows, LANES), jnp.float32)
    x[:, :, LANES + cols :] = jnp.zeros((layers, rows, LANES), jnp.float32)

    def part_at(s, place):
        away = jnp.where(lax.rem(s, 2) == 0, s // 2, PARTS - (s + 1) // 2)
        return lax.rem(place // per + PARTS // 2 + away, PARTS)

    def rows_copy(side):
        return pltpu.make_async_remote_copy(
            src_ref=rows_out.at[1 - side],
            dst_ref=rows_in.at[side],
            send_sem=rows_ss.at[side],
            recv_sem=rows_rs.at[side],
            device_id=(me, down if side == 0 else up),
            device_id_type=MESH,
        )

    def depth_copy(side, s, place, gx):
        start = pl.multiple_of(part_at(s, place) * width, width)
        return pltpu.make_async_remote_copy(
            src_ref=density.at[layers - 1 if side == 0 else 0, :, pl.ds(start, width)],
            dst_ref=depth_in.at[side, :, pl.ds(start, width)],
            send_sem=depth_ss.at[side, s],
            recv_sem=depth_rs.at[side, s],
            device_id=(gx, my),
            device_id_type=MESH,
        )

    def p1_copy(s, k):
        to = lax.rem(y + k, Q)
        return pltpu.make_async_remote_copy(
            src_ref=p1s.at[s, to],
            dst_ref=p1r.at[s, k],
            send_sem=p1_ss.at[s, k],
            recv_sem=p1_rs.at[s, k],
            device_id=(z * Q + to, my),
            device_id_type=MESH,
        )

    def last_copy(g, k):
        at, to = lax.rem(in_group + g, per), lax.rem(y + k, Q)
        return pltpu.make_async_remote_copy(
            src_ref=p1s.at[PARTS - 1, to, at],
            dst_ref=lastr.at[g, k],
            send_sem=last_ss.at[g, k],
            recv_sem=last_rs.at[g, k],
            device_id=((first_z + at) * Q + to, my),
            device_id_type=MESH,
        )

    def p2_copy(k):
        to = lax.rem(z + k, nz)
        return pltpu.make_async_remote_copy(
            src_ref=p2s.at[to],
            dst_ref=p2r.at[k],
            send_sem=p2_ss.at[k],
            recv_sem=p2_rs.at[k],
            device_id=(to * Q + y, my),
            device_id_type=MESH,
        )

    for fetch in fetches:
        fetch.wait()
    tile = (8, LANES)
    scale = math.sqrt(math.log2(math.e))
    for k in range(bumps):
        weight = jnp.full(tile, weights[k] * step_size, jnp.float32)
        prm[6 * k] = jnp.full(tile, centers[k], jnp.float32)
        prm[6 * k + 1] = scale / jnp.full(tile, widths[k], jnp.float32)
        prm[6 * k + 2] = jnp.log2(weight)
        for c in range(3):
            prm[6 * k + 3 + c] = jnp.full(tile, colors[c, k], jnp.float32) / weight
    for c in range(3):
        prm[6 * bumps + c] = jnp.full(tile, 0.5 * light[c], jnp.float32)

    load.wait()
    for l in range(layers):
        rows_out[0, l : l + 1, :] = x[l, 0:1, LANES : LANES + cols]
        rows_out[1, l : l + 1, :] = x[l, rows - 1 : rows, LANES : LANES + cols]

    lane = lax.broadcasted_iota(jnp.int32, tile, 1)
    row = lax.broadcasted_iota(jnp.int32, tile, 0)
    lane_all = lax.broadcasted_iota(jnp.int32, (rows, LANES), 1)
    from_prv = jnp.where(me > 0, 1.0, 0.0).astype(jnp.float32)
    from_nxt = jnp.where(me < nx - 1, 1.0, 0.0).astype(jnp.float32)
    from_up = jnp.where(my > 0, 1.0, 0.0).astype(jnp.float32)
    from_down = jnp.where(my < ny - 1, 1.0, 0.0).astype(jnp.float32)
    reps = (rows // 8, SUB // LANES)

    def wide(i):
        return jnp.tile(prm[i], reps)

    def emit(s):
        part = part_at(s, z)

        def one(i, _):
            l, start = lax.rem(i, layers), (i // layers) * SUB
            cells = x[l, :, pl.ds(pl.multiple_of(part * width + start + LANES, LANES), SUB)]
            sums = None
            for k in range(bumps):
                scaled = (cells - wide(6 * k)) * wide(6 * k + 1)
                step = jnp.exp2(wide(6 * k + 2) - scaled * scaled)
                terms = [step] + [step * wide(6 * k + 3 + c) for c in range(3)]
                sums = terms if sums is None else [a + b for a, b in zip(sums, terms)]
            t = sums[0]
            opacity = t * (1.0 - t * (0.5 - t * (1.0 / 6.0 - t * (1.0 / 24.0))))
            at = pl.ds(pl.multiple_of(start, SUB), SUB)
            for c, v in enumerate([opacity] + sums[1:]):
                emi[s, c, l, :, at] = v
            return 0

        lax.fori_loop(0, layers * (width // SUB), one, 0)

    n_lane, n_row = SUB // LANES, rows // 8

    def grid_of(v):
        return [[v[8 * r : 8 * r + 8, LANES * c : LANES * c + LANES] for c in range(v.shape[1] // LANES)] for r in range(v.shape[0] // 8)]

    def joined(tiles):
        return jnp.concatenate([jnp.concatenate(line, 1) for line in tiles], 0)

    def march(s):
        part = part_at(s, z)

        def one(i, _):
            at = pl.multiple_of(part * width + i * SUB, SUB)
            here = pl.ds(pl.multiple_of(i * SUB, SUB), SUB)
            hx, hy, hz = (wide(6 * bumps + c) for c in range(3))
            clear = jnp.ones((rows, SUB), jnp.float32)
            opaque = jnp.zeros((rows, SUB), jnp.float32)
            colour = [jnp.zeros((rows, SUB), jnp.float32) for c in range(3)]

            def layer(l):
                return x[l, :, pl.ds(pl.multiple_of(at + LANES, LANES), SUB)]

            before, cells = depth_in[0, :, pl.ds(at, SUB)] * from_prv, layer(0)
            for l in range(layers):
                after = layer(l + 1) if l < layers - 1 else depth_in[1, :, pl.ds(at, SUB)] * from_nxt
                tiles = grid_of(cells)
                left = grid_of(x[l, :, pl.ds(at, LANES)])
                right = grid_of(x[l, :, pl.ds(pl.multiple_of(at + LANES + SUB, LANES), LANES)])
                behind = [shifted(tiles[r], 1, roll_lanes(left[r][0], 1), lane, 1) for r in range(n_row)]
                ahead = [shifted(tiles[r], -1, roll_lanes(right[r][0], -1), lane, 1) for r in range(n_row)]
                over_row = jnp.broadcast_to(rows_in[0, l : l + 1, pl.ds(at, SUB)], (8, SUB)) * from_up
                under_row = jnp.broadcast_to(rows_in[1, l : l + 1, pl.ds(at, SUB)], (8, SUB)) * from_down
                above, below = [], []
                for c in range(n_lane):
                    column = [tiles[r][c] for r in range(n_row)]
                    above.append(shifted(column, 1, over_row[:, LANES * c : LANES * c + LANES], row, 0))
                    below.append(shifted(column, -1, under_row[:, LANES * c : LANES * c + LANES], row, 0))
                above = [[above[c][r] for c in range(n_lane)] for r in range(n_row)]
                below = [[below[c][r] for c in range(n_lane)] for r in range(n_row)]
                facing = (
                    hx * (after - before)
                    + hy * (joined(below) - joined(above))
                    + hz * (joined(ahead) - joined(behind))
                )
                shading = 0.625 + 0.375 * jnp.tanh(facing)
                seen = clear * emi[s, 0, l, :, here]
                clear, opaque = clear - seen, opaque + seen
                lit = seen * shading
                colour = [colour[c] + lit * emi[s, c + 1, l, :, here] for c in range(3)]
                before, cells = cells, after
            for b in range(n_lane):
                cut = slice(LANES * b, LANES * b + LANES)
                owned = regroup([v[:, cut] for v in colour + [opaque]], lane_all)
                for j in range(Q):
                    p1s[s, j, i * n_lane + b] = owned[j]
            return 0

        lax.fori_loop(0, width // SUB, one, 0)

    emit(0)
    pl.semaphore_wait(barrier, 4 + (nz - 1) + per * (Q - 1))

    def send_depth(s):
        depth_copy(0, s, nxt // Q, nxt).start()
        depth_copy(1, s, prv // Q, prv).start()

    send_depth(0)
    for side in range(2):
        rows_copy(side).start()
    for s in range(1, LEAD):
        send_depth(s)
    for s in range(1, LEAD):
        emit(s)
    for side in range(2):
        rows_copy(side).wait_recv()


    def step(s, _):
        @pl.when((s >= LEAD) & (s < PARTS))
        def _():
            emit(s)

        @pl.when(s < PARTS)
        def _():
            @pl.when(s + LEAD < PARTS)
            def _():
                send_depth(s + LEAD)

            for side in range(2):
                depth_copy(side, s, z, (nxt, prv)[side]).wait_recv()
            march(s)

        @pl.when(s < PARTS - 1)
        def _():
            for k in (2, 1, 3):
                p1_copy(s, k).start()

        @pl.when(s == PARTS - 1)
        def _():
            for g in range(per):
                for k in range(Q):
                    if (g, k) != (0, 0):
                        last_copy(g, k).start()

        @pl.when(s >= 2)
        def _():
            t = s - 2
            first = part_at(t, z) * per
            p1r[t, 0] = p1s[t, y]
            for k in range(1, Q):
                p1_copy(t, k).wait_recv()
            flat = (per * rows, LANES)
            lane_flat = lax.broadcasted_iota(jnp.int32, flat, 1)
            total = p1r[t, lax.rem(y + 1, Q)].reshape(flat)
            for j in range(Q - 2, -1, -1):
                total = over(p1r[t, lax.rem(y + Q - j, Q)].reshape(flat), total, lane_flat)
            total = total.reshape(per, rows, LANES)
            for b in range(per):
                p2s[first + b] = total[b]
                p2_copy(lax.rem(first + b + nz - z, nz)).start()

        return 0

    lax.fori_loop(0, PARTS + 1, step, 0)

    for side in range(2):
        rows_copy(side).wait_send()

    def finish(s, _):
        for side in range(2):
            depth_copy(side, s, z, (nxt, prv)[side]).wait_send()

        @pl.when(s < PARTS - 1)
        def _():
            for k in range(1, Q):
                p1_copy(s, k).wait_send()

        return 0

    lax.fori_loop(0, PARTS, finish, 0)

    lastr[0, 0] = p1s[PARTS - 1, y, in_group]
    for g in range(per):
        for k in range(Q):
            if (g, k) != (0, 0):
                last_copy(g, k).wait()
    for g in range(per):
        near = lax.rem(in_group + per - g, per)
        total = lastr[near, lax.rem(y + 1, Q)]
        for j in range(Q - 2, -1, -1):
            total = over(lastr[near, lax.rem(y + Q - j, Q)], total, lane_all)
        p2r[lax.rem(z + nz - (first_z + g), nz)] = total

    def finish_p2(i, _):
        other = lax.rem(first_z + i, nz)
        p2_copy(lax.rem(other + nz - z, nz)).wait_send()
        p2_copy(lax.rem(z + nz - other, nz)).wait_recv()
        return 0

    lax.fori_loop(per, nz, finish_p2, 0)

    total = p2r[lax.rem(z + 1, nz)]
    for i in range(1, nz):
        total = over(p2r[lax.rem(z + 1 + i, nz)], total, lane_all)
    for c in range(4):
        out[c] = total[:, G * c : G * c + G]


def local(nx, ny, density, centers, widths, weights, colors, light):
    layers, rows, cols = density.shape
    nz, bumps = nx // Q, centers.shape[0]
    width = cols // PARTS
    per = width // LANES
    dma = pltpu.SemaphoreType.DMA
    hbm = pl.BlockSpec(memory_space=pltpu.HBM)
    f32 = jnp.float32
    return pl.pallas_call(
        functools.partial(kernel, nx, ny, 1.5 / (layers * nx)),
        out_shape=jax.ShapeDtypeStruct((4, rows, cols // nx), f32),
        in_specs=[hbm] * 6,
        out_specs=pl.BlockSpec(memory_space=pltpu.VMEM),
        scratch_shapes=[pltpu.SMEM(given.shape, f32) for given in (centers, widths, weights, colors, light)]
        + [
            pltpu.VMEM((layers, rows, cols + 2 * LANES), f32),
            pltpu.VMEM((2, layers, cols), f32),
            pltpu.VMEM((2, layers, cols), f32),
            pltpu.VMEM((2, rows, cols), f32),
            pltpu.VMEM((6 * bumps + 3, 8, LANES), f32),
            pltpu.VMEM((PARTS, 4, layers, rows, width), f32),
            pltpu.VMEM((PARTS, Q, per, rows, LANES), f32),
            pltpu.VMEM((PARTS - 1, Q, per, rows, LANES), f32),
            pltpu.VMEM((per, Q, rows, LANES), f32),
            pltpu.VMEM((nz, rows, LANES), f32),
            pltpu.VMEM((nz, rows, LANES), f32),
            dma,
            dma((5,)),
            dma((2,)),
            dma((2,)),
            dma((2, PARTS)),
            dma((2, PARTS)),
            dma((PARTS - 1, Q)),
            dma((PARTS - 1, Q)),
            dma((per, Q)),
            dma((per, Q)),
            dma((nz,)),
            dma((nz,)),
        ],
        compiler_params=pltpu.CompilerParams(
            collective_id=0, has_side_effects=True, vmem_limit_bytes=40 * 1024 * 1024
        ),
        cost_estimate=pl.CostEstimate(
            flops=130 * density.size, bytes_accessed=4 * density.size, transcendentals=9 * density.size
        ),
    )(*(pltpu.with_memory_space_constraint(v, pltpu.HBM) for v in (density, centers, widths, weights, colors, light)))


def solution(mesh):
    nx, ny = mesh.shape["gx"], mesh.shape["gy"]
    in_specs = (P("gx", "gy", None), P(), P(), P(), P(), P())
    out_specs = P(None, "gy", "gx")
    return jax.shard_map(
        functools.partial(local, nx, ny), mesh=mesh, in_specs=in_specs, out_specs=out_specs, check_vma=False
    )
```

```python
import functools
import math

import jax
import jax.numpy as jnp
from jax import lax
from jax.experimental import pallas as pl
from jax.experimental.pallas import tpu as pltpu
from jax.sharding import PartitionSpec as P

MESH = pl.DeviceIdType.MESH
LANES = 128
Q = 4
G = LANES // Q
PARTS = 8
LEAD = 2


def roll_lanes(v, by):
    return pltpu.roll(v, by % LANES, axis=1)


def shifted(tiles, by, edge, lane_or_row, axis):
    size = tiles[0].shape[axis]
    if by > 0:
        ahead, at = [edge] + tiles[:-1], size - 1
    else:
        ahead, at = tiles[1:] + [edge], 0
    return [pltpu.roll(jnp.where(lane_or_row == at, a, t), by % size, axis=axis) for a, t in zip(ahead, tiles)]


def regroup(values, lane):
    a, b, c, d = values
    low = lane < 2 * G
    ac0 = jnp.where(low, a, roll_lanes(c, 2 * G))
    ac1 = jnp.where(low, roll_lanes(a, -2 * G), c)
    bd0 = jnp.where(low, b, roll_lanes(d, 2 * G))
    bd1 = jnp.where(low, roll_lanes(b, -2 * G), d)
    even = lax.rem(lane // G, 2) == 0
    out = []
    for first, second in ((ac0, bd0), (ac1, bd1)):
        out.append(jnp.where(even, first, roll_lanes(second, G)))
        out.append(jnp.where(even, roll_lanes(first, -G), second))
    return out


def over(front, back, lane):
    clear = 1.0 - front
    ends = jnp.where(lane < G, roll_lanes(clear, G), clear)
    inner = (lane >= G) & (lane < 3 * G)
    return front + jnp.where(inner, roll_lanes(ends, 2 * G), ends) * back


def kernel(
    nx, ny, step_size, density, *rest,
):
    given, rest = rest[:5], rest[5:]
    out, centers, widths, weights, colors, light = rest[:6]
    x, rows_out, rows_in, depth_in, prm, emi, p1s, p1r, lastr, p2s, p2r = rest[6:17]
    x_sem, given_sem, rows_ss, rows_rs, depth_ss, depth_rs, p1_ss, p1_rs, last_ss, last_rs, p2_ss, p2_rs = rest[17:]
    layers, rows, cols = density.shape
    nz = nx // Q
    bumps = centers.shape[0]
    width = cols // PARTS
    per = width // LANES
    me, my = lax.axis_index("gx"), lax.axis_index("gy")
    z, y = me // Q, lax.rem(me, Q)
    first_z, in_group = z // per * per, lax.rem(z, per)
    nxt, prv = lax.rem(me + 1, nx), lax.rem(me + nx - 1, nx)
    down, up = lax.rem(my + 1, ny), lax.rem(my + ny - 1, ny)

    load = pltpu.make_async_copy(density, x.at[:, :, pl.ds(LANES, cols)], x_sem)
    load.start()
    fetches = [
        pltpu.make_async_copy(src, dst, given_sem.at[i])
        for i, (src, dst) in enumerate(zip(given, (centers, widths, weights, colors, light)))
    ]
    for fetch in fetches:
        fetch.start()

    barrier = pltpu.get_barrier_semaphore()

    def greet(gx, gy):
        pl.semaphore_signal(barrier, inc=1, device_id=(gx, gy), device_id_type=MESH)

    greet(nxt, my)
    greet(prv, my)
    greet(me, down)
    greet(me, up)

    def greet_z(k, _):
        greet(lax.rem(z + k, nz) * Q + y, my)
        return 0

    lax.fori_loop(1, nz, greet_z, 0)
    for k in range(1, Q):
        for g in range(per):
            greet((first_z + lax.rem(in_group + g, per)) * Q + lax.rem(y + k, Q), my)
    x[:, :, :LANES] = jnp.zeros((layers, rows, LANES), jnp.float32)
    x[:, :, LANES + cols :] = jnp.zeros((layers, rows, LANES), jnp.float32)

    def part_at(s, place):
        away = jnp.where(lax.rem(s, 2) == 0, s // 2, PARTS - (s + 1) // 2)
        return lax.rem(place // per + PARTS // 2 + away, PARTS)

    def rows_copy(side):
        return pltpu.make_async_remote_copy(
            src_ref=rows_out.at[1 - side],
            dst_ref=rows_in.at[side],
            send_sem=rows_ss.at[side],
            recv_sem=rows_rs.at[side],
            device_id=(me, down if side == 0 else up),
            device_id_type=MESH,
        )

    def depth_copy(side, s, place, gx):
        start = pl.multiple_of(part_at(s, place) * width, width)
        return pltpu.make_async_remote_copy(
            src_ref=density.at[layers - 1 if side == 0 else 0, :, pl.ds(start, width)],
            dst_ref=depth_in.at[side, :, pl.ds(start, width)],
            send_sem=depth_ss.at[side, s],
            recv_sem=depth_rs.at[side, s],
            device_id=(gx, my),
            device_id_type=MESH,
        )

    def p1_copy(s, k):
        to = lax.rem(y + k, Q)
        return pltpu.make_async_remote_copy(
            src_ref=p1s.at[s, to],
            dst_ref=p1r.at[s, k],
            send_sem=p1_ss.at[s, k],
            recv_sem=p1_rs.at[s, k],
            device_id=(z * Q + to, my),
            device_id_type=MESH,
        )

    def last_copy(g, k):
        at, to = lax.rem(in_group + g, per), lax.rem(y + k, Q)
        return pltpu.make_async_remote_copy(
            src_ref=p1s.at[PARTS - 1, to, at],
            dst_ref=lastr.at[g, k],
            send_sem=last_ss.at[g, k],
            recv_sem=last_rs.at[g, k],
            device_id=((first_z + at) * Q + to, my),
            device_id_type=MESH,
        )

    def p2_copy(k):
        to = lax.rem(z + k, nz)
        return pltpu.make_async_remote_copy(
            src_ref=p2s.at[to],
            dst_ref=p2r.at[k],
            send_sem=p2_ss.at[k],
            recv_sem=p2_rs.at[k],
            device_id=(to * Q + y, my),
            device_id_type=MESH,
        )

    for fetch in fetches:
        fetch.wait()
    tile = (8, LANES)
    scale = math.sqrt(math.log2(math.e))
    for k in range(bumps):
        weight = jnp.full(tile, weights[k] * step_size, jnp.float32)
        prm[6 * k] = jnp.full(tile, centers[k], jnp.float32)
        prm[6 * k + 1] = scale / jnp.full(tile, widths[k], jnp.float32)
        prm[6 * k + 2] = jnp.log2(weight)
        for c in range(3):
            prm[6 * k + 3 + c] = jnp.full(tile, colors[c, k], jnp.float32) / weight
    for c in range(3):
        prm[6 * bumps + c] = jnp.full(tile, 0.5 * light[c], jnp.float32)

    load.wait()
    for l in range(layers):
        rows_out[0, l : l + 1, :] = x[l, 0:1, LANES : LANES + cols]
        rows_out[1, l : l + 1, :] = x[l, rows - 1 : rows, LANES : LANES + cols]

    lane = lax.broadcasted_iota(jnp.int32, tile, 1)
    row = lax.broadcasted_iota(jnp.int32, tile, 0)
    lane_all = lax.broadcasted_iota(jnp.int32, (rows, LANES), 1)
    from_prv = jnp.where(me > 0, 1.0, 0.0).astype(jnp.float32)
    from_nxt = jnp.where(me < nx - 1, 1.0, 0.0).astype(jnp.float32)
    from_up = jnp.where(my > 0, 1.0, 0.0).astype(jnp.float32)
    from_down = jnp.where(my < ny - 1, 1.0, 0.0).astype(jnp.float32)
    n_row = rows // 8

    def wide(i):
        return jnp.concatenate([prm[i]] * n_row, 0)

    def split(v):
        return [v[8 * r : 8 * r + 8] for r in range(n_row)]

    def column_of(s, i):
        return pl.multiple_of(part_at(s, z) * width + i * LANES, LANES)

    def emit_layer(s, i, at, l):
        cells = x[l, :, pl.ds(pl.multiple_of(at + LANES, LANES), LANES)]
        sums = None
        for k in range(bumps):
            scaled = (cells - wide(6 * k)) * wide(6 * k + 1)
            step = jnp.exp2(wide(6 * k + 2) - scaled * scaled)
            terms = [step] + [step * wide(6 * k + 3 + c) for c in range(3)]
            sums = terms if sums is None else [a + b for a, b in zip(sums, terms)]
        t = sums[0]
        opacity = t * (1.0 - t * (0.5 - t * (1.0 / 6.0 - t * (1.0 / 24.0))))
        for c, v in enumerate([opacity] + sums[1:]):
            emi[s, i, l, c] = v

    def march_layer(s, i, at, l, state):
        clear, opaque, colour = state
        here = pl.ds(at, LANES)

        def layer(n):
            return x[n, :, pl.ds(pl.multiple_of(at + LANES, LANES), LANES)]

        before = layer(l - 1) if l > 0 else depth_in[0, :, here] * from_prv
        after = layer(l + 1) if l < layers - 1 else depth_in[1, :, here] * from_nxt
        tiles = split(layer(l))
        left = split(x[l, :, pl.ds(at, LANES)])
        right = split(x[l, :, pl.ds(pl.multiple_of(at + 2 * LANES, LANES), LANES)])
        over_row = jnp.broadcast_to(rows_in[0, l : l + 1, here], tile) * from_up
        under_row = jnp.broadcast_to(rows_in[1, l : l + 1, here], tile) * from_down
        behind = [shifted([t], 1, e, lane, 1)[0] for t, e in zip(tiles, left)]
        ahead = [shifted([t], -1, e, lane, 1)[0] for t, e in zip(tiles, right)]
        above = shifted(tiles, 1, over_row, row, 0)
        below = shifted(tiles, -1, under_row, row, 0)
        hx, hy, hz = (wide(6 * bumps + c) for c in range(3))
        facing = (
            hx * (after - before)
            + hy * jnp.concatenate([b - a for a, b in zip(above, below)], 0)
            + hz * jnp.concatenate([b - a for a, b in zip(behind, ahead)], 0)
        )
        shading = 0.625 + 0.375 * jnp.tanh(facing)
        seen = clear * emi[s, i, l, 0]
        lit = seen * shading
        return clear - seen, opaque + seen, [colour[c] + lit * emi[s, i, l, c + 1] for c in range(3)]

    def march_end(s, i, state):
        owned = regroup(state[2] + [state[1]], lane_all)
        for j in range(Q):
            p1s[s, j, i] = owned[j]

    zero = jnp.zeros((rows, LANES), jnp.float32)
    fresh = (jnp.ones((rows, LANES), jnp.float32), zero, [zero] * 3)

    def emit(s):
        def one(n, _):
            i, l = lax.rem(n, per), n // per * 2
            at = column_of(s, i)
            emit_layer(s, i, at, l)
            emit_layer(s, i, at, l + 1)
            return 0

        lax.fori_loop(0, per * layers // 2, one, 0)

    def march(s):
        def one(i, _):
            at, state = column_of(s, i), fresh
            for l in range(layers):
                state = march_layer(s, i, at, l, state)
            march_end(s, i, state)
            return 0

        lax.fori_loop(0, per, one, 0)

    def emit_and_march(e, s):
        def one(i, _):
            emit_at, at, state = column_of(e, i), column_of(s, i), fresh
            for l in range(layers):
                emit_layer(e, i, emit_at, l)
                state = march_layer(s, i, at, l, state)
            march_end(s, i, state)
            return 0

        lax.fori_loop(0, per, one, 0)

    emit(0)
    pl.semaphore_wait(barrier, 4 + (nz - 1) + per * (Q - 1))

    def send_depth(s):
        depth_copy(0, s, nxt // Q, nxt).start()
        depth_copy(1, s, prv // Q, prv).start()

    send_depth(0)
    for side in range(2):
        rows_copy(side).start()
    for s in range(1, LEAD):
        send_depth(s)
    for s in range(1, LEAD):
        emit(s)
    for side in range(2):
        rows_copy(side).wait_recv()


    def step(s, _):
        @pl.when(s < PARTS)
        def _():
            for side in range(2):
                depth_copy(side, s, z, (nxt, prv)[side]).wait_recv()

        @pl.when(s + LEAD < PARTS)
        def _():
            send_depth(s + LEAD)
            emit_and_march(s + LEAD, s)

        @pl.when((s + LEAD >= PARTS) & (s < PARTS))
        def _():
            march(s)

        @pl.when(s < PARTS - 1)
        def _():
            for k in (2, 1, 3):
                p1_copy(s, k).start()

        @pl.when(s == PARTS - 1)
        def _():
            for g in range(per):
                for k in range(Q):
                    if (g, k) != (0, 0):
                        last_copy(g, k).start()

        @pl.when(s >= 2)
        def _():
            t = s - 2
            first = part_at(t, z) * per
            p1r[t, 0] = p1s[t, y]
            for k in range(1, Q):
                p1_copy(t, k).wait_recv()
            flat = (per * rows, LANES)
            lane_flat = lax.broadcasted_iota(jnp.int32, flat, 1)
            total = p1r[t, lax.rem(y + 1, Q)].reshape(flat)
            for j in range(Q - 2, -1, -1):
                total = over(p1r[t, lax.rem(y + Q - j, Q)].reshape(flat), total, lane_flat)
            total = total.reshape(per, rows, LANES)
            for b in range(per):
                p2s[first + b] = total[b]
                p2_copy(lax.rem(first + b + nz - z, nz)).start()

        return 0

    lax.fori_loop(0, PARTS + 1, step, 0)

    for side in range(2):
        rows_copy(side).wait_send()

    def finish(s, _):
        for side in range(2):
            depth_copy(side, s, z, (nxt, prv)[side]).wait_send()

        @pl.when(s < PARTS - 1)
        def _():
            for k in range(1, Q):
                p1_copy(s, k).wait_send()

        return 0

    lax.fori_loop(0, PARTS, finish, 0)

    lastr[0, 0] = p1s[PARTS - 1, y, in_group]
    for g in range(per):
        for k in range(Q):
            if (g, k) != (0, 0):
                last_copy(g, k).wait()
    for g in range(per):
        near = lax.rem(in_group + per - g, per)
        total = lastr[near, lax.rem(y + 1, Q)]
        for j in range(Q - 2, -1, -1):
            total = over(lastr[near, lax.rem(y + Q - j, Q)], total, lane_all)
        p2r[lax.rem(z + nz - (first_z + g), nz)] = total

    def finish_p2(i, _):
        other = lax.rem(first_z + i, nz)
        p2_copy(lax.rem(other + nz - z, nz)).wait_send()
        p2_copy(lax.rem(z + nz - other, nz)).wait_recv()
        return 0

    lax.fori_loop(per, nz, finish_p2, 0)

    total = p2r[lax.rem(z + 1, nz)]
    for i in range(1, nz):
        total = over(p2r[lax.rem(z + 1 + i, nz)], total, lane_all)
    for c in range(4):
        out[c] = total[:, G * c : G * c + G]


def local(nx, ny, density, centers, widths, weights, colors, light):
    layers, rows, cols = density.shape
    nz, bumps = nx // Q, centers.shape[0]
    width = cols // PARTS
    per = width // LANES
    dma = pltpu.SemaphoreType.DMA
    hbm = pl.BlockSpec(memory_space=pltpu.HBM)
    f32 = jnp.float32
    return pl.pallas_call(
        functools.partial(kernel, nx, ny, 1.5 / (layers * nx)),
        out_shape=jax.ShapeDtypeStruct((4, rows, cols // nx), f32),
        in_specs=[hbm] * 6,
        out_specs=pl.BlockSpec(memory_space=pltpu.VMEM),
        scratch_shapes=[pltpu.SMEM(given.shape, f32) for given in (centers, widths, weights, colors, light)]
        + [
            pltpu.VMEM((layers, rows, cols + 2 * LANES), f32),
            pltpu.VMEM((2, layers, cols), f32),
            pltpu.VMEM((2, layers, cols), f32),
            pltpu.VMEM((2, rows, cols), f32),
            pltpu.VMEM((6 * bumps + 3, 8, LANES), f32),
            pltpu.VMEM((PARTS, per, layers, 4, rows, LANES), f32),
            pltpu.VMEM((PARTS, Q, per, rows, LANES), f32),
            pltpu.VMEM((PARTS - 1, Q, per, rows, LANES), f32),
            pltpu.VMEM((per, Q, rows, LANES), f32),
            pltpu.VMEM((nz, rows, LANES), f32),
            pltpu.VMEM((nz, rows, LANES), f32),
            dma,
            dma((5,)),
            dma((2,)),
            dma((2,)),
            dma((2, PARTS)),
            dma((2, PARTS)),
            dma((PARTS - 1, Q)),
            dma((PARTS - 1, Q)),
            dma((per, Q)),
            dma((per, Q)),
            dma((nz,)),
            dma((nz,)),
        ],
        compiler_params=pltpu.CompilerParams(
            collective_id=0, has_side_effects=True, vmem_limit_bytes=40 * 1024 * 1024
        ),
        cost_estimate=pl.CostEstimate(
            flops=130 * density.size, bytes_accessed=4 * density.size, transcendentals=9 * density.size
        ),
    )(*(pltpu.with_memory_space_constraint(v, pltpu.HBM) for v in (density, centers, widths, weights, colors, light)))


def solution(mesh):
    nx, ny = mesh.shape["gx"], mesh.shape["gy"]
    in_specs = (P("gx", "gy", None), P(), P(), P(), P(), P())
    out_specs = P(None, "gy", "gx")
    return jax.shard_map(
        functools.partial(local, nx, ny), mesh=mesh, in_specs=in_specs, out_specs=out_specs, check_vma=False
    )
```

```python
import functools
import math

import jax
import jax.numpy as jnp
from jax import lax
from jax.experimental import pallas as pl
from jax.experimental.pallas import tpu as pltpu
from jax.sharding import PartitionSpec as P

MESH = pl.DeviceIdType.MESH
LANES = 128
Q = 4
G = LANES // Q
PARTS = 8
LEAD = 2


def roll_lanes(v, by):
    return pltpu.roll(v, by % LANES, axis=1)


def shifted(tiles, by, edge, lane_or_row, axis):
    size = tiles[0].shape[axis]
    if by > 0:
        ahead, at = [edge] + tiles[:-1], size - 1
    else:
        ahead, at = tiles[1:] + [edge], 0
    return [pltpu.roll(jnp.where(lane_or_row == at, a, t), by % size, axis=axis) for a, t in zip(ahead, tiles)]


def regroup(values, lane):
    a, b, c, d = values
    low = lane < 2 * G
    ac0 = jnp.where(low, a, roll_lanes(c, 2 * G))
    ac1 = jnp.where(low, roll_lanes(a, -2 * G), c)
    bd0 = jnp.where(low, b, roll_lanes(d, 2 * G))
    bd1 = jnp.where(low, roll_lanes(b, -2 * G), d)
    even = lax.rem(lane // G, 2) == 0
    out = []
    for first, second in ((ac0, bd0), (ac1, bd1)):
        out.append(jnp.where(even, first, roll_lanes(second, G)))
        out.append(jnp.where(even, roll_lanes(first, -G), second))
    return out


def over(front, back, lane):
    clear = 1.0 - front
    ends = jnp.where(lane < G, roll_lanes(clear, G), clear)
    inner = (lane >= G) & (lane < 3 * G)
    return front + jnp.where(inner, roll_lanes(ends, 2 * G), ends) * back


def kernel(
    nx, ny, step_size, density, *rest,
):
    given, rest = rest[:5], rest[5:]
    out, centers, widths, weights, colors, light = rest[:6]
    x, rows_out, rows_in, depth_in, prm, emi, p1s, p1r, lastr, p2s, p2r = rest[6:17]
    x_sem, given_sem, rows_ss, rows_rs, depth_ss, depth_rs, p1_ss, p1_rs, last_ss, last_rs, p2_ss, p2_rs = rest[17:]
    layers, rows, cols = density.shape
    nz = nx // Q
    bumps = centers.shape[0]
    width = cols // PARTS
    per = width // LANES
    me, my = lax.axis_index("gx"), lax.axis_index("gy")
    z, y = me // Q, lax.rem(me, Q)
    first_z, in_group = z // per * per, lax.rem(z, per)
    nxt, prv = lax.rem(me + 1, nx), lax.rem(me + nx - 1, nx)
    down, up = lax.rem(my + 1, ny), lax.rem(my + ny - 1, ny)

    load = pltpu.make_async_copy(density, x.at[:, :, pl.ds(LANES, cols)], x_sem)
    load.start()
    fetches = [
        pltpu.make_async_copy(src, dst, given_sem.at[i])
        for i, (src, dst) in enumerate(zip(given, (centers, widths, weights, colors, light)))
    ]
    for fetch in fetches:
        fetch.start()

    barrier = pltpu.get_barrier_semaphore()

    def greet(gx, gy):
        pl.semaphore_signal(barrier, inc=1, device_id=(gx, gy), device_id_type=MESH)

    greet(nxt, my)
    greet(prv, my)
    greet(me, down)
    greet(me, up)

    def greet_z(k, _):
        greet(lax.rem(z + k, nz) * Q + y, my)
        return 0

    lax.fori_loop(1, nz, greet_z, 0)
    for k in range(1, Q):
        for g in range(per):
            greet((first_z + lax.rem(in_group + g, per)) * Q + lax.rem(y + k, Q), my)
    x[:, :, :LANES] = jnp.zeros((layers, rows, LANES), jnp.float32)
    x[:, :, LANES + cols :] = jnp.zeros((layers, rows, LANES), jnp.float32)

    def part_at(s, place):
        away = jnp.where(lax.rem(s, 2) == 0, s // 2, PARTS - (s + 1) // 2)
        return lax.rem(place // per + PARTS // 2 + away, PARTS)

    def rows_copy(side):
        return pltpu.make_async_remote_copy(
            src_ref=rows_out.at[1 - side],
            dst_ref=rows_in.at[side],
            send_sem=rows_ss.at[side],
            recv_sem=rows_rs.at[side],
            device_id=(me, down if side == 0 else up),
            device_id_type=MESH,
        )

    def depth_copy(side, s, place, gx):
        start = pl.multiple_of(part_at(s, place) * width, width)
        return pltpu.make_async_remote_copy(
            src_ref=density.at[layers - 1 if side == 0 else 0, :, pl.ds(start, width)],
            dst_ref=depth_in.at[side, :, pl.ds(start, width)],
            send_sem=depth_ss.at[side, s],
            recv_sem=depth_rs.at[side, s],
            device_id=(gx, my),
            device_id_type=MESH,
        )

    def p1_copy(s, k):
        to = lax.rem(y + k, Q)
        return pltpu.make_async_remote_copy(
            src_ref=p1s.at[s, to],
            dst_ref=p1r.at[s, k],
            send_sem=p1_ss.at[s, k],
            recv_sem=p1_rs.at[s, k],
            device_id=(z * Q + to, my),
            device_id_type=MESH,
        )

    def last_copy(g, k):
        at, to = lax.rem(in_group + g, per), lax.rem(y + k, Q)
        return pltpu.make_async_remote_copy(
            src_ref=p1s.at[PARTS - 1, to, at],
            dst_ref=lastr.at[g, k],
            send_sem=last_ss.at[g, k],
            recv_sem=last_rs.at[g, k],
            device_id=((first_z + at) * Q + to, my),
            device_id_type=MESH,
        )

    def p2_copy(k):
        to = lax.rem(z + k, nz)
        return pltpu.make_async_remote_copy(
            src_ref=p2s.at[to],
            dst_ref=p2r.at[k],
            send_sem=p2_ss.at[k],
            recv_sem=p2_rs.at[k],
            device_id=(to * Q + y, my),
            device_id_type=MESH,
        )

    for fetch in fetches:
        fetch.wait()
    tile = (8, LANES)
    scale = math.sqrt(math.log2(math.e))
    for k in range(bumps):
        weight = jnp.full(tile, weights[k] * step_size, jnp.float32)
        prm[6 * k] = jnp.full(tile, centers[k], jnp.float32)
        prm[6 * k + 1] = scale / jnp.full(tile, widths[k], jnp.float32)
        prm[6 * k + 2] = jnp.log2(weight)
        for c in range(3):
            prm[6 * k + 3 + c] = jnp.full(tile, colors[c, k], jnp.float32) / weight
    for c in range(3):
        prm[6 * bumps + c] = jnp.full(tile, 0.5 * light[c], jnp.float32)

    load.wait()
    for l in range(layers):
        rows_out[0, l : l + 1, :] = x[l, 0:1, LANES : LANES + cols]
        rows_out[1, l : l + 1, :] = x[l, rows - 1 : rows, LANES : LANES + cols]

    lane = lax.broadcasted_iota(jnp.int32, tile, 1)
    row = lax.broadcasted_iota(jnp.int32, tile, 0)
    lane_all = lax.broadcasted_iota(jnp.int32, (rows, LANES), 1)
    from_prv = jnp.where(me > 0, 1.0, 0.0).astype(jnp.float32)
    from_nxt = jnp.where(me < nx - 1, 1.0, 0.0).astype(jnp.float32)
    from_up = jnp.where(my > 0, 1.0, 0.0).astype(jnp.float32)
    from_down = jnp.where(my < ny - 1, 1.0, 0.0).astype(jnp.float32)
    n_row = rows // 8

    def wide(i):
        return jnp.concatenate([prm[i]] * n_row, 0)

    def split(v):
        return [v[8 * r : 8 * r + 8] for r in range(n_row)]

    def column_of(s, i):
        return pl.multiple_of(part_at(s, z) * width + i * LANES, LANES)

    def emit_layer(s, i, at, l):
        cells = x[l, :, pl.ds(pl.multiple_of(at + LANES, LANES), LANES)]
        sums = None
        for k in range(bumps):
            scaled = (cells - wide(6 * k)) * wide(6 * k + 1)
            step = jnp.exp2(wide(6 * k + 2) - scaled * scaled)
            terms = [step] + [step * wide(6 * k + 3 + c) for c in range(3)]
            sums = terms if sums is None else [a + b for a, b in zip(sums, terms)]
        t = sums[0]
        opacity = t * (1.0 - t * (0.5 - t * (1.0 / 6.0 - t * (1.0 / 24.0))))
        for c, v in enumerate([opacity] + sums[1:]):
            emi[s, i, l, c] = v

    def march_layer(s, i, at, l, state):
        clear, opaque, colour = state
        here = pl.ds(at, LANES)

        def layer(n):
            return x[n, :, pl.ds(pl.multiple_of(at + LANES, LANES), LANES)]

        before = layer(l - 1) if l > 0 else depth_in[0, :, here] * from_prv
        after = layer(l + 1) if l < layers - 1 else depth_in[1, :, here] * from_nxt
        tiles = split(layer(l))
        left = split(x[l, :, pl.ds(at, LANES)])
        right = split(x[l, :, pl.ds(pl.multiple_of(at + 2 * LANES, LANES), LANES)])
        over_row = jnp.broadcast_to(rows_in[0, l : l + 1, here], tile) * from_up
        under_row = jnp.broadcast_to(rows_in[1, l : l + 1, here], tile) * from_down
        behind = [shifted([t], 1, e, lane, 1)[0] for t, e in zip(tiles, left)]
        ahead = [shifted([t], -1, e, lane, 1)[0] for t, e in zip(tiles, right)]
        above = shifted(tiles, 1, over_row, row, 0)
        below = shifted(tiles, -1, under_row, row, 0)
        hx, hy, hz = (wide(6 * bumps + c) for c in range(3))
        facing = (
            hx * (after - before)
            + hy * jnp.concatenate([b - a for a, b in zip(above, below)], 0)
            + hz * jnp.concatenate([b - a for a, b in zip(behind, ahead)], 0)
        )
        shading = 0.625 + 0.375 * jnp.tanh(facing)
        seen = clear * emi[s, i, l, 0]
        lit = seen * shading
        return clear - seen, opaque + seen, [colour[c] + lit * emi[s, i, l, c + 1] for c in range(3)]

    def march_end(s, i, state):
        owned = regroup(state[2] + [state[1]], lane_all)
        for j in range(Q):
            p1s[s, j, i] = owned[j]

    zero = jnp.zeros((rows, LANES), jnp.float32)
    fresh = (jnp.ones((rows, LANES), jnp.float32), zero, [zero] * 3)

    def emit(s):
        def one(n, _):
            i, l = lax.rem(n, per), n // per * 2
            at = column_of(s, i)
            emit_layer(s, i, at, l)
            emit_layer(s, i, at, l + 1)
            return 0

        lax.fori_loop(0, per * layers // 2, one, 0)

    def march(s):
        def one(i, _):
            at, state = column_of(s, i), fresh
            for l in range(layers):
                state = march_layer(s, i, at, l, state)
            march_end(s, i, state)
            return 0

        lax.fori_loop(0, per, one, 0)

    def emit_and_march(e, s):
        def one(i, _):
            emit_at, at, state = column_of(e, i), column_of(s, i), fresh
            for l in range(layers):
                emit_layer(e, i, emit_at, l)
                state = march_layer(s, i, at, l, state)
            march_end(s, i, state)
            return 0

        lax.fori_loop(0, per, one, 0)

    emit(0)
    pl.semaphore_wait(barrier, 4 + (nz - 1) + per * (Q - 1))

    def send_depth(s):
        depth_copy(0, s, nxt // Q, nxt).start()
        depth_copy(1, s, prv // Q, prv).start()

    send_depth(0)
    for side in range(2):
        rows_copy(side).start()
    for s in range(1, LEAD):
        send_depth(s)
    for s in range(1, LEAD):
        emit(s)

    def send_more(s, _):
        send_depth(s)
        return 0

    lax.fori_loop(LEAD, PARTS, send_more, 0)
    for side in range(2):
        rows_copy(side).wait_recv()


    def step(s, _):
        @pl.when(s < PARTS)
        def _():
            for side in range(2):
                depth_copy(side, s, z, (nxt, prv)[side]).wait_recv()

        @pl.when(s + LEAD < PARTS)
        def _():
            emit_and_march(s + LEAD, s)

        @pl.when((s + LEAD >= PARTS) & (s < PARTS))
        def _():
            march(s)

        @pl.when(s < PARTS - 1)
        def _():
            for k in (2, 1, 3):
                p1_copy(s, k).start()

        @pl.when(s == PARTS - 1)
        def _():
            for g in range(per):
                for k in range(Q):
                    if (g, k) != (0, 0):
                        last_copy(g, k).start()

        @pl.when(s >= 2)
        def _():
            t = s - 2
            first = part_at(t, z) * per
            p1r[t, 0] = p1s[t, y]
            for k in range(1, Q):
                p1_copy(t, k).wait_recv()
            flat = (per * rows, LANES)
            lane_flat = lax.broadcasted_iota(jnp.int32, flat, 1)
            total = p1r[t, lax.rem(y + 1, Q)].reshape(flat)
            for j in range(Q - 2, -1, -1):
                total = over(p1r[t, lax.rem(y + Q - j, Q)].reshape(flat), total, lane_flat)
            total = total.reshape(per, rows, LANES)
            for b in range(per):
                p2s[first + b] = total[b]
                p2_copy(lax.rem(first + b + nz - z, nz)).start()

        return 0

    lax.fori_loop(0, PARTS + 1, step, 0)

    for side in range(2):
        rows_copy(side).wait_send()

    def finish(s, _):
        for side in range(2):
            depth_copy(side, s, z, (nxt, prv)[side]).wait_send()

        @pl.when(s < PARTS - 1)
        def _():
            for k in range(1, Q):
                p1_copy(s, k).wait_send()

        return 0

    lax.fori_loop(0, PARTS, finish, 0)

    lastr[0, 0] = p1s[PARTS - 1, y, in_group]
    for g in range(per):
        for k in range(Q):
            if (g, k) != (0, 0):
                last_copy(g, k).wait()
    for g in range(per):
        near = lax.rem(in_group + per - g, per)
        total = lastr[near, lax.rem(y + 1, Q)]
        for j in range(Q - 2, -1, -1):
            total = over(lastr[near, lax.rem(y + Q - j, Q)], total, lane_all)
        p2r[lax.rem(z + nz - (first_z + g), nz)] = total

    def finish_p2(i, _):
        other = lax.rem(first_z + i, nz)
        p2_copy(lax.rem(other + nz - z, nz)).wait_send()
        p2_copy(lax.rem(z + nz - other, nz)).wait_recv()
        return 0

    lax.fori_loop(per, nz, finish_p2, 0)

    total = p2r[lax.rem(z + 1, nz)]
    for i in range(1, nz):
        total = over(p2r[lax.rem(z + 1 + i, nz)], total, lane_all)
    for c in range(4):
        out[c] = total[:, G * c : G * c + G]


def local(nx, ny, density, centers, widths, weights, colors, light):
    layers, rows, cols = density.shape
    nz, bumps = nx // Q, centers.shape[0]
    width = cols // PARTS
    per = width // LANES
    dma = pltpu.SemaphoreType.DMA
    hbm = pl.BlockSpec(memory_space=pltpu.HBM)
    f32 = jnp.float32
    return pl.pallas_call(
        functools.partial(kernel, nx, ny, 1.5 / (layers * nx)),
        out_shape=jax.ShapeDtypeStruct((4, rows, cols // nx), f32),
        in_specs=[hbm] * 6,
        out_specs=pl.BlockSpec(memory_space=pltpu.VMEM),
        scratch_shapes=[pltpu.SMEM(given.shape, f32) for given in (centers, widths, weights, colors, light)]
        + [
            pltpu.VMEM((layers, rows, cols + 2 * LANES), f32),
            pltpu.VMEM((2, layers, cols), f32),
            pltpu.VMEM((2, layers, cols), f32),
            pltpu.VMEM((2, rows, cols), f32),
            pltpu.VMEM((6 * bumps + 3, 8, LANES), f32),
            pltpu.VMEM((PARTS, per, layers, 4, rows, LANES), f32),
            pltpu.VMEM((PARTS, Q, per, rows, LANES), f32),
            pltpu.VMEM((PARTS - 1, Q, per, rows, LANES), f32),
            pltpu.VMEM((per, Q, rows, LANES), f32),
            pltpu.VMEM((nz, rows, LANES), f32),
            pltpu.VMEM((nz, rows, LANES), f32),
            dma,
            dma((5,)),
            dma((2,)),
            dma((2,)),
            dma((2, PARTS)),
            dma((2, PARTS)),
            dma((PARTS - 1, Q)),
            dma((PARTS - 1, Q)),
            dma((per, Q)),
            dma((per, Q)),
            dma((nz,)),
            dma((nz,)),
        ],
        compiler_params=pltpu.CompilerParams(
            collective_id=0, has_side_effects=True, vmem_limit_bytes=40 * 1024 * 1024
        ),
        cost_estimate=pl.CostEstimate(
            flops=130 * density.size, bytes_accessed=4 * density.size, transcendentals=9 * density.size
        ),
    )(*(pltpu.with_memory_space_constraint(v, pltpu.HBM) for v in (density, centers, widths, weights, colors, light)))


def solution(mesh):
    nx, ny = mesh.shape["gx"], mesh.shape["gy"]
    in_specs = (P("gx", "gy", None), P(), P(), P(), P(), P())
    out_specs = P(None, "gy", "gx")
    return jax.shard_map(
        functools.partial(local, nx, ny), mesh=mesh, in_specs=in_specs, out_specs=out_specs, check_vma=False
    )
```

```python
import functools
import math

import jax
import jax.numpy as jnp
from jax import lax
from jax.experimental import pallas as pl
from jax.experimental.pallas import tpu as pltpu
from jax.sharding import PartitionSpec as P

MESH = pl.DeviceIdType.MESH
LANES = 128
Q = 4
G = LANES // Q
PARTS = 8
LEAD = 2
PASSED = 5


def roll_lanes(v, by):
    return pltpu.roll(v, by % LANES, axis=1)


def shifted(tiles, by, edge, lane_or_row, axis):
    size = tiles[0].shape[axis]
    if by > 0:
        ahead, at = [edge] + tiles[:-1], size - 1
    else:
        ahead, at = tiles[1:] + [edge], 0
    return [pltpu.roll(jnp.where(lane_or_row == at, a, t), by % size, axis=axis) for a, t in zip(ahead, tiles)]


def regroup(values, lane):
    a, b, c, d = values
    low = lane < 2 * G
    ac0 = jnp.where(low, a, roll_lanes(c, 2 * G))
    ac1 = jnp.where(low, roll_lanes(a, -2 * G), c)
    bd0 = jnp.where(low, b, roll_lanes(d, 2 * G))
    bd1 = jnp.where(low, roll_lanes(b, -2 * G), d)
    even = lax.rem(lane // G, 2) == 0
    out = []
    for first, second in ((ac0, bd0), (ac1, bd1)):
        out.append(jnp.where(even, first, roll_lanes(second, G)))
        out.append(jnp.where(even, roll_lanes(first, -G), second))
    return out


def over(front, back, lane):
    clear = 1.0 - front
    ends = jnp.where(lane < G, roll_lanes(clear, G), clear)
    inner = (lane >= G) & (lane < 3 * G)
    return front + jnp.where(inner, roll_lanes(ends, 2 * G), ends) * back


def kernel(
    nx, ny, step_size, density, *rest,
):
    given, rest = rest[:5], rest[5:]
    out, centers, widths, weights, colors, light = rest[:6]
    x, rows_out, rows_in, depth_in, prm, emi, p1s, p1r, passed, lastr, p2s, p2r = rest[6:18]
    x_sem, given_sem, rows_ss, rows_rs, depth_ss, depth_rs, p1_ss, p1_rs, pass_ss, pass_rs, last_ss, last_rs, p2_ss, p2_rs = rest[18:]
    layers, rows, cols = density.shape
    nz = nx // Q
    bumps = centers.shape[0]
    width = cols // PARTS
    per = width // LANES
    me, my = lax.axis_index("gx"), lax.axis_index("gy")
    z, y = me // Q, lax.rem(me, Q)
    first_z, in_group = z // per * per, lax.rem(z, per)
    nxt, prv = lax.rem(me + 1, nx), lax.rem(me + nx - 1, nx)
    down, up = lax.rem(my + 1, ny), lax.rem(my + ny - 1, ny)

    load = pltpu.make_async_copy(density, x.at[:, :, pl.ds(LANES, cols)], x_sem)
    load.start()
    fetches = [
        pltpu.make_async_copy(src, dst, given_sem.at[i])
        for i, (src, dst) in enumerate(zip(given, (centers, widths, weights, colors, light)))
    ]
    for fetch in fetches:
        fetch.start()

    barrier = pltpu.get_barrier_semaphore()

    def greet(gx, gy):
        pl.semaphore_signal(barrier, inc=1, device_id=(gx, gy), device_id_type=MESH)

    greet(nxt, my)
    greet(prv, my)
    greet(me, down)
    greet(me, up)

    def greet_z(k, _):
        greet(lax.rem(z + k, nz) * Q + y, my)
        return 0

    lax.fori_loop(1, nz, greet_z, 0)
    for k in range(1, Q):
        for g in range(per):
            greet((first_z + lax.rem(in_group + g, per)) * Q + lax.rem(y + k, Q), my)
    x[:, :, :LANES] = jnp.zeros((layers, rows, LANES), jnp.float32)
    x[:, :, LANES + cols :] = jnp.zeros((layers, rows, LANES), jnp.float32)

    def part_at(s, place):
        away = jnp.where(lax.rem(s, 2) == 0, s // 2, PARTS - (s + 1) // 2)
        return lax.rem(place // per + PARTS // 2 + away, PARTS)

    def rows_copy(side):
        return pltpu.make_async_remote_copy(
            src_ref=rows_out.at[1 - side],
            dst_ref=rows_in.at[side],
            send_sem=rows_ss.at[side],
            recv_sem=rows_rs.at[side],
            device_id=(me, down if side == 0 else up),
            device_id_type=MESH,
        )

    def depth_copy(side, s, place, gx):
        start = pl.multiple_of(part_at(s, place) * width, width)
        return pltpu.make_async_remote_copy(
            src_ref=density.at[layers - 1 if side == 0 else 0, :, pl.ds(start, width)],
            dst_ref=depth_in.at[side, :, pl.ds(start, width)],
            send_sem=depth_ss.at[side, s],
            recv_sem=depth_rs.at[side, s],
            device_id=(gx, my),
            device_id_type=MESH,
        )

    def p1_copy(s, k):
        to = lax.rem(y + k, Q)
        return pltpu.make_async_remote_copy(
            src_ref=p1s.at[s, to],
            dst_ref=p1r.at[s, k],
            send_sem=p1_ss.at[s, k],
            recv_sem=p1_rs.at[s, k],
            device_id=(z * Q + to, my),
            device_id_type=MESH,
        )

    def far_copy(s):
        to = lax.rem(y + 2, Q)
        return pltpu.make_async_remote_copy(
            src_ref=p1s.at[s, to, 0],
            dst_ref=p1r.at[s, 2, 0],
            send_sem=p1_ss.at[s, 2],
            recv_sem=p1_rs.at[s, 2],
            device_id=(z * Q + to, my),
            device_id_type=MESH,
        )

    def pass_copy(s, leg):
        return pltpu.make_async_remote_copy(
            src_ref=p1s.at[s, lax.rem(y + 2, Q), pl.ds(1, per - 1)] if leg == 0 else passed.at[s],
            dst_ref=passed.at[s] if leg == 0 else p1r.at[s, 2, pl.ds(1, per - 1)],
            send_sem=pass_ss.at[leg, s],
            recv_sem=pass_rs.at[leg, s],
            device_id=(z * Q + lax.rem(y + Q - 1, Q), my),
            device_id_type=MESH,
        )

    def last_copy(g, k):
        at, to = lax.rem(in_group + g, per), lax.rem(y + k, Q)
        return pltpu.make_async_remote_copy(
            src_ref=p1s.at[PARTS - 1, to, at],
            dst_ref=lastr.at[g, k],
            send_sem=last_ss.at[g, k],
            recv_sem=last_rs.at[g, k],
            device_id=((first_z + at) * Q + to, my),
            device_id_type=MESH,
        )

    def p2_copy(k):
        to = lax.rem(z + k, nz)
        return pltpu.make_async_remote_copy(
            src_ref=p2s.at[to],
            dst_ref=p2r.at[k],
            send_sem=p2_ss.at[k],
            recv_sem=p2_rs.at[k],
            device_id=(to * Q + y, my),
            device_id_type=MESH,
        )

    for fetch in fetches:
        fetch.wait()
    tile = (8, LANES)
    scale = math.sqrt(math.log2(math.e))
    for k in range(bumps):
        weight = jnp.full(tile, weights[k] * step_size, jnp.float32)
        prm[6 * k] = jnp.full(tile, centers[k], jnp.float32)
        prm[6 * k + 1] = scale / jnp.full(tile, widths[k], jnp.float32)
        prm[6 * k + 2] = jnp.log2(weight)
        for c in range(3):
            prm[6 * k + 3 + c] = jnp.full(tile, colors[c, k], jnp.float32) / weight
    for c in range(3):
        prm[6 * bumps + c] = jnp.full(tile, 0.5 * light[c], jnp.float32)

    load.wait()
    for l in range(layers):
        rows_out[0, l : l + 1, :] = x[l, 0:1, LANES : LANES + cols]
        rows_out[1, l : l + 1, :] = x[l, rows - 1 : rows, LANES : LANES + cols]

    lane = lax.broadcasted_iota(jnp.int32, tile, 1)
    row = lax.broadcasted_iota(jnp.int32, tile, 0)
    lane_all = lax.broadcasted_iota(jnp.int32, (rows, LANES), 1)
    from_prv = jnp.where(me > 0, 1.0, 0.0).astype(jnp.float32)
    from_nxt = jnp.where(me < nx - 1, 1.0, 0.0).astype(jnp.float32)
    from_up = jnp.where(my > 0, 1.0, 0.0).astype(jnp.float32)
    from_down = jnp.where(my < ny - 1, 1.0, 0.0).astype(jnp.float32)
    n_row = rows // 8

    def wide(i):
        return jnp.concatenate([prm[i]] * n_row, 0)

    def split(v):
        return [v[8 * r : 8 * r + 8] for r in range(n_row)]

    def column_of(s, i):
        return pl.multiple_of(part_at(s, z) * width + i * LANES, LANES)

    def emit_layer(s, i, at, l):
        cells = x[l, :, pl.ds(pl.multiple_of(at + LANES, LANES), LANES)]
        sums = None
        for k in range(bumps):
            scaled = (cells - wide(6 * k)) * wide(6 * k + 1)
            step = jnp.exp2(wide(6 * k + 2) - scaled * scaled)
            terms = [step] + [step * wide(6 * k + 3 + c) for c in range(3)]
            sums = terms if sums is None else [a + b for a, b in zip(sums, terms)]
        t = sums[0]
        opacity = t * (1.0 - t * (0.5 - t * (1.0 / 6.0 - t * (1.0 / 24.0))))
        for c, v in enumerate([opacity] + sums[1:]):
            emi[s, i, l, c] = v

    def march_layer(s, i, at, l, state):
        clear, opaque, colour = state
        here = pl.ds(at, LANES)

        def layer(n):
            return x[n, :, pl.ds(pl.multiple_of(at + LANES, LANES), LANES)]

        before = layer(l - 1) if l > 0 else depth_in[0, :, here] * from_prv
        after = layer(l + 1) if l < layers - 1 else depth_in[1, :, here] * from_nxt
        tiles = split(layer(l))
        left = split(x[l, :, pl.ds(at, LANES)])
        right = split(x[l, :, pl.ds(pl.multiple_of(at + 2 * LANES, LANES), LANES)])
        over_row = jnp.broadcast_to(rows_in[0, l : l + 1, here], tile) * from_up
        under_row = jnp.broadcast_to(rows_in[1, l : l + 1, here], tile) * from_down
        behind = [shifted([t], 1, e, lane, 1)[0] for t, e in zip(tiles, left)]
        ahead = [shifted([t], -1, e, lane, 1)[0] for t, e in zip(tiles, right)]
        above = shifted(tiles, 1, over_row, row, 0)
        below = shifted(tiles, -1, under_row, row, 0)
        hx, hy, hz = (wide(6 * bumps + c) for c in range(3))
        facing = (
            hx * (after - before)
            + hy * jnp.concatenate([b - a for a, b in zip(above, below)], 0)
            + hz * jnp.concatenate([b - a for a, b in zip(behind, ahead)], 0)
        )
        shading = 0.625 + 0.375 * jnp.tanh(facing)
        seen = clear * emi[s, i, l, 0]
        lit = seen * shading
        return clear - seen, opaque + seen, [colour[c] + lit * emi[s, i, l, c + 1] for c in range(3)]

    def march_end(s, i, state):
        owned = regroup(state[2] + [state[1]], lane_all)
        for j in range(Q):
            p1s[s, j, i] = owned[j]

    zero = jnp.zeros((rows, LANES), jnp.float32)
    fresh = (jnp.ones((rows, LANES), jnp.float32), zero, [zero] * 3)

    def emit(s):
        def one(n, _):
            i, l = lax.rem(n, per), n // per * 2
            at = column_of(s, i)
            emit_layer(s, i, at, l)
            emit_layer(s, i, at, l + 1)
            return 0

        lax.fori_loop(0, per * layers // 2, one, 0)

    def pass_on(s, i):
        @pl.when((i == 1) & (s >= 2) & (s < PASSED + 2))
        def _():
            pass_copy(s - 2, 0).wait_recv()
            pass_copy(s - 2, 1).start()

    def march(s):
        def one(i, _):
            pass_on(s, i)
            at, state = column_of(s, i), fresh
            for l in range(layers):
                state = march_layer(s, i, at, l, state)
            march_end(s, i, state)
            return 0

        lax.fori_loop(0, per, one, 0)

    def emit_and_march(e, s):
        def one(i, _):
            pass_on(s, i)
            emit_at, at, state = column_of(e, i), column_of(s, i), fresh
            for l in range(layers):
                emit_layer(e, i, emit_at, l)
                state = march_layer(s, i, at, l, state)
            march_end(s, i, state)
            return 0

        lax.fori_loop(0, per, one, 0)

    emit(0)
    pl.semaphore_wait(barrier, 4 + (nz - 1) + per * (Q - 1))

    def send_depth(s):
        depth_copy(0, s, nxt // Q, nxt).start()
        depth_copy(1, s, prv // Q, prv).start()

    send_depth(0)
    for side in range(2):
        rows_copy(side).start()
    for s in range(1, LEAD):
        send_depth(s)
    for s in range(1, LEAD):
        emit(s)

    def send_more(s, _):
        send_depth(s)
        return 0

    lax.fori_loop(LEAD, PARTS, send_more, 0)
    for side in range(2):
        rows_copy(side).wait_recv()


    def step(s, _):
        @pl.when(s < PARTS)
        def _():
            for side in range(2):
                depth_copy(side, s, z, (nxt, prv)[side]).wait_recv()

        @pl.when(s + LEAD < PARTS)
        def _():
            emit_and_march(s + LEAD, s)

        @pl.when((s + LEAD >= PARTS) & (s < PARTS))
        def _():
            march(s)

        @pl.when(s < PARTS - 1)
        def _():
            @pl.when(s < PASSED)
            def _():
                pass_copy(s, 0).start()
                far_copy(s).start()

            @pl.when(s >= PASSED)
            def _():
                p1_copy(s, 2).start()

            for k in (1, 3):
                p1_copy(s, k).start()

        @pl.when(s == PARTS - 1)
        def _():
            for g in range(per):
                for k in range(Q):
                    if (g, k) != (0, 0):
                        last_copy(g, k).start()

        @pl.when(s >= 3)
        def _():
            t = s - 3
            first = part_at(t, z) * per
            p1r[t, 0] = p1s[t, y]
            for k in (1, 3):
                p1_copy(t, k).wait_recv()

            @pl.when(t < PASSED)
            def _():
                far_copy(t).wait_recv()
                pass_copy(t, 1).wait_recv()

            @pl.when(t >= PASSED)
            def _():
                p1_copy(t, 2).wait_recv()

            flat = (per * rows, LANES)
            lane_flat = lax.broadcasted_iota(jnp.int32, flat, 1)
            total = p1r[t, lax.rem(y + 1, Q)].reshape(flat)
            for j in range(Q - 2, -1, -1):
                total = over(p1r[t, lax.rem(y + Q - j, Q)].reshape(flat), total, lane_flat)
            total = total.reshape(per, rows, LANES)
            for b in range(per):
                p2s[first + b] = total[b]
                p2_copy(lax.rem(first + b + nz - z, nz)).start()

        return 0

    lax.fori_loop(0, PARTS + 2, step, 0)

    for side in range(2):
        rows_copy(side).wait_send()

    def finish(s, _):
        for side in range(2):
            depth_copy(side, s, z, (nxt, prv)[side]).wait_send()

        @pl.when(s < PARTS - 1)
        def _():
            for k in (1, 3):
                p1_copy(s, k).wait_send()

            @pl.when(s < PASSED)
            def _():
                far_copy(s).wait_send()
                for leg in range(2):
                    pass_copy(s, leg).wait_send()

            @pl.when(s >= PASSED)
            def _():
                p1_copy(s, 2).wait_send()

        return 0

    lax.fori_loop(0, PARTS, finish, 0)

    lastr[0, 0] = p1s[PARTS - 1, y, in_group]
    for g in range(per):
        for k in range(Q):
            if (g, k) != (0, 0):
                last_copy(g, k).wait()
    for g in range(per):
        near = lax.rem(in_group + per - g, per)
        total = lastr[near, lax.rem(y + 1, Q)]
        for j in range(Q - 2, -1, -1):
            total = over(lastr[near, lax.rem(y + Q - j, Q)], total, lane_all)
        p2r[lax.rem(z + nz - (first_z + g), nz)] = total

    def finish_p2(i, _):
        other = lax.rem(first_z + i, nz)
        p2_copy(lax.rem(other + nz - z, nz)).wait_send()
        p2_copy(lax.rem(z + nz - other, nz)).wait_recv()
        return 0

    lax.fori_loop(per, nz, finish_p2, 0)

    total = p2r[lax.rem(z + 1, nz)]
    for i in range(1, nz):
        total = over(p2r[lax.rem(z + 1 + i, nz)], total, lane_all)
    for c in range(4):
        out[c] = total[:, G * c : G * c + G]


def local(nx, ny, density, centers, widths, weights, colors, light):
    layers, rows, cols = density.shape
    nz, bumps = nx // Q, centers.shape[0]
    width = cols // PARTS
    per = width // LANES
    dma = pltpu.SemaphoreType.DMA
    hbm = pl.BlockSpec(memory_space=pltpu.HBM)
    f32 = jnp.float32
    return pl.pallas_call(
        functools.partial(kernel, nx, ny, 1.5 / (layers * nx)),
        out_shape=jax.ShapeDtypeStruct((4, rows, cols // nx), f32),
        in_specs=[hbm] * 6,
        out_specs=pl.BlockSpec(memory_space=pltpu.VMEM),
        scratch_shapes=[pltpu.SMEM(given.shape, f32) for given in (centers, widths, weights, colors, light)]
        + [
            pltpu.VMEM((layers, rows, cols + 2 * LANES), f32),
            pltpu.VMEM((2, layers, cols), f32),
            pltpu.VMEM((2, layers, cols), f32),
            pltpu.VMEM((2, rows, cols), f32),
            pltpu.VMEM((6 * bumps + 3, 8, LANES), f32),
            pltpu.VMEM((PARTS, per, layers, 4, rows, LANES), f32),
            pltpu.VMEM((PARTS, Q, per, rows, LANES), f32),
            pltpu.VMEM((PARTS - 1, Q, per, rows, LANES), f32),
            pltpu.VMEM((PASSED, per - 1, rows, LANES), f32),
            pltpu.VMEM((per, Q, rows, LANES), f32),
            pltpu.VMEM((nz, rows, LANES), f32),
            pltpu.VMEM((nz, rows, LANES), f32),
            dma,
            dma((5,)),
            dma((2,)),
            dma((2,)),
            dma((2, PARTS)),
            dma((2, PARTS)),
            dma((PARTS - 1, Q)),
            dma((PARTS - 1, Q)),
            dma((2, PASSED)),
            dma((2, PASSED)),
            dma((per, Q)),
            dma((per, Q)),
            dma((nz,)),
            dma((nz,)),
        ],
        compiler_params=pltpu.CompilerParams(
            collective_id=0, has_side_effects=True, vmem_limit_bytes=40 * 1024 * 1024
        ),
        cost_estimate=pl.CostEstimate(
            flops=130 * density.size, bytes_accessed=4 * density.size, transcendentals=9 * density.size
        ),
    )(*(pltpu.with_memory_space_constraint(v, pltpu.HBM) for v in (density, centers, widths, weights, colors, light)))


def solution(mesh):
    nx, ny = mesh.shape["gx"], mesh.shape["gy"]
    in_specs = (P("gx", "gy", None), P(), P(), P(), P(), P())
    out_specs = P(None, "gy", "gx")
    return jax.shard_map(
        functools.partial(local, nx, ny), mesh=mesh, in_specs=in_specs, out_specs=out_specs, check_vma=False
    )
```

```python
import functools
import math

import jax
import jax.numpy as jnp
from jax import lax
from jax.experimental import pallas as pl
from jax.experimental.pallas import tpu as pltpu
from jax.sharding import PartitionSpec as P

MESH = pl.DeviceIdType.MESH
LANES = 128
Q = 4
DEEP = 256
G = LANES // Q
PARTS = 8
LEAD = 2


def roll_lanes(v, by):
    return pltpu.roll(v, by % LANES, axis=1)


def shifted(tiles, by, edge, lane_or_row, axis):
    size = tiles[0].shape[axis]
    if by > 0:
        ahead, at = [edge] + tiles[:-1], size - 1
    else:
        ahead, at = tiles[1:] + [edge], 0
    return [pltpu.roll(jnp.where(lane_or_row == at, a, t), by % size, axis=axis) for a, t in zip(ahead, tiles)]


def regroup(values, lane):
    a, b, c, d = values
    low = lane < 2 * G
    ac0 = jnp.where(low, a, roll_lanes(c, 2 * G))
    ac1 = jnp.where(low, roll_lanes(a, -2 * G), c)
    bd0 = jnp.where(low, b, roll_lanes(d, 2 * G))
    bd1 = jnp.where(low, roll_lanes(b, -2 * G), d)
    even = lax.rem(lane // G, 2) == 0
    out = []
    for first, second in ((ac0, bd0), (ac1, bd1)):
        out.append(jnp.where(even, first, roll_lanes(second, G)))
        out.append(jnp.where(even, roll_lanes(first, -G), second))
    return out


def over(front, back, lane):
    clear = 1.0 - front
    ends = jnp.where(lane < G, roll_lanes(clear, G), clear)
    inner = (lane >= G) & (lane < 3 * G)
    return front + jnp.where(inner, roll_lanes(ends, 2 * G), ends) * back


def kernel(
    nx, ny, step_size, density, *rest,
):
    given, rest = rest[:5], rest[5:]
    out, centers, widths, weights, colors, light = rest[:6]
    x, rows_out, rows_in, depth_in, prm, mix, emi, p1s, p1r, lastr, p2s, p2r = rest[6:18]
    x_sem, given_sem, rows_ss, rows_rs, depth_ss, depth_rs, p1_ss, p1_rs, last_ss, last_rs, p2_ss, p2_rs = rest[18:]
    layers, rows, cols = density.shape
    nz = nx // Q
    bumps = centers.shape[0]
    width = cols // PARTS
    per = width // LANES
    me, my = lax.axis_index("gx"), lax.axis_index("gy")
    z, y = me // Q, lax.rem(me, Q)
    first_z, in_group = z // per * per, lax.rem(z, per)
    nxt, prv = lax.rem(me + 1, nx), lax.rem(me + nx - 1, nx)
    down, up = lax.rem(my + 1, ny), lax.rem(my + ny - 1, ny)

    load = pltpu.make_async_copy(density, x.at[:, :, pl.ds(LANES, cols)], x_sem)
    load.start()
    fetches = [
        pltpu.make_async_copy(src, dst, given_sem.at[i])
        for i, (src, dst) in enumerate(zip(given, (centers, widths, weights, colors, light)))
    ]
    for fetch in fetches:
        fetch.start()

    barrier = pltpu.get_barrier_semaphore()

    def greet(gx, gy):
        pl.semaphore_signal(barrier, inc=1, device_id=(gx, gy), device_id_type=MESH)

    greet(nxt, my)
    greet(prv, my)
    greet(me, down)
    greet(me, up)

    def greet_z(k, _):
        greet(lax.rem(z + k, nz) * Q + y, my)
        return 0

    lax.fori_loop(1, nz, greet_z, 0)
    for k in range(1, Q):
        for g in range(per):
            greet((first_z + lax.rem(in_group + g, per)) * Q + lax.rem(y + k, Q), my)
    x[:, :, :LANES] = jnp.zeros((layers, rows, LANES), jnp.float32)
    x[:, :, LANES + cols :] = jnp.zeros((layers, rows, LANES), jnp.float32)

    def part_at(s, place):
        away = jnp.where(lax.rem(s, 2) == 0, s // 2, PARTS - (s + 1) // 2)
        return lax.rem(place // per + PARTS // 2 + away, PARTS)

    def rows_copy(side):
        return pltpu.make_async_remote_copy(
            src_ref=rows_out.at[1 - side],
            dst_ref=rows_in.at[side],
            send_sem=rows_ss.at[side],
            recv_sem=rows_rs.at[side],
            device_id=(me, down if side == 0 else up),
            device_id_type=MESH,
        )

    def depth_copy(side, s, place, gx):
        start = pl.multiple_of(part_at(s, place) * width, width)
        return pltpu.make_async_remote_copy(
            src_ref=density.at[layers - 1 if side == 0 else 0, :, pl.ds(start, width)],
            dst_ref=depth_in.at[side, :, pl.ds(start, width)],
            send_sem=depth_ss.at[side, s],
            recv_sem=depth_rs.at[side, s],
            device_id=(gx, my),
            device_id_type=MESH,
        )

    def p1_copy(s, k):
        to = lax.rem(y + k, Q)
        return pltpu.make_async_remote_copy(
            src_ref=p1s.at[s, to],
            dst_ref=p1r.at[s, k],
            send_sem=p1_ss.at[s, k],
            recv_sem=p1_rs.at[s, k],
            device_id=(z * Q + to, my),
            device_id_type=MESH,
        )

    def last_copy(g, k):
        at, to = lax.rem(in_group + g, per), lax.rem(y + k, Q)
        return pltpu.make_async_remote_copy(
            src_ref=p1s.at[PARTS - 1, to, at],
            dst_ref=lastr.at[g, k],
            send_sem=last_ss.at[g, k],
            recv_sem=last_rs.at[g, k],
            device_id=((first_z + at) * Q + to, my),
            device_id_type=MESH,
        )

    def p2_copy(k):
        to = lax.rem(z + k, nz)
        return pltpu.make_async_remote_copy(
            src_ref=p2s.at[to],
            dst_ref=p2r.at[k],
            send_sem=p2_ss.at[k],
            recv_sem=p2_rs.at[k],
            device_id=(to * Q + y, my),
            device_id_type=MESH,
        )

    for fetch in fetches:
        fetch.wait()
    tile = (8, LANES)
    scale = math.sqrt(math.log2(math.e))
    for k in range(bumps):
        inverse = scale / jnp.full(tile, widths[k], jnp.float32)
        prm[2 * k] = jnp.full(tile, centers[k], jnp.float32)
        prm[2 * k + 1] = -inverse * inverse
    for c in range(3):
        prm[2 * bumps + c] = jnp.full(tile, 0.5 * light[c], jnp.float32)
    into = lax.broadcasted_iota(jnp.int32, (rows, DEEP), 0)
    out_of = lax.broadcasted_iota(jnp.int32, (rows, DEEP), 1)
    lines = []
    for c in range(4):
        line = jnp.zeros((rows, DEEP), jnp.float32)
        for k in range(bumps):
            factor = weights[k] * step_size if c == 0 else colors[c - 1, k] * 0.375
            line = jnp.where(out_of == into + k * rows, factor, line)
        lines.append(line)
    exact = jnp.concatenate(lines, 0)
    high = exact.astype(jnp.bfloat16)
    mix[: 4 * rows] = high
    mix[4 * rows :] = (exact - high.astype(jnp.float32)).astype(jnp.bfloat16)

    load.wait()
    for l in range(layers):
        rows_out[0, l : l + 1, :] = x[l, 0:1, LANES : LANES + cols]
        rows_out[1, l : l + 1, :] = x[l, rows - 1 : rows, LANES : LANES + cols]

    lane = lax.broadcasted_iota(jnp.int32, tile, 1)
    row = lax.broadcasted_iota(jnp.int32, tile, 0)
    lane_all = lax.broadcasted_iota(jnp.int32, (rows, LANES), 1)
    from_prv = jnp.where(me > 0, 1.0, 0.0).astype(jnp.float32)
    from_nxt = jnp.where(me < nx - 1, 1.0, 0.0).astype(jnp.float32)
    from_up = jnp.where(my > 0, 1.0, 0.0).astype(jnp.float32)
    from_down = jnp.where(my < ny - 1, 1.0, 0.0).astype(jnp.float32)
    n_row = rows // 8

    def wide(i):
        return jnp.concatenate([prm[i]] * n_row, 0)

    def split(v):
        return [v[8 * r : 8 * r + 8] for r in range(n_row)]

    def column_of(s, i):
        return pl.multiple_of(part_at(s, z) * width + i * LANES, LANES)

    def broad(i):
        return jnp.concatenate([wide(i)] * per, 1)

    def emit_layer(s, l):
        cells = x[l, :, pl.ds(pl.multiple_of(part_at(s, z) * width + LANES, LANES), width)]
        stack = []
        for k in range(bumps):
            away = cells - broad(2 * k)
            stack.append(jnp.exp2(away * away * broad(2 * k + 1)))
        if DEEP > bumps * rows:
            stack.append(jnp.zeros((DEEP - bumps * rows, width), jnp.float32))
        exact = jnp.concatenate(stack, 0)
        high = exact.astype(jnp.bfloat16)
        low = (exact - high.astype(jnp.float32)).astype(jnp.bfloat16)
        most = jnp.dot(mix[...], high, preferred_element_type=jnp.float32)
        rest = jnp.dot(mix[: 4 * rows], low, preferred_element_type=jnp.float32)
        sums = most[: 4 * rows] + (most[4 * rows :] + rest)
        t = sums[:rows]
        opacity = t * (1.0 - t * (0.5 - t * (1.0 / 6.0 - t * (1.0 / 24.0))))
        emi[s, l, 0] = opacity
        for c in range(1, 4):
            emi[s, l, c] = sums[c * rows : (c + 1) * rows]

    def march_layer(s, i, at, l, state):
        clear, opaque, colour = state
        here = pl.ds(at, LANES)

        def layer(n):
            return x[n, :, pl.ds(pl.multiple_of(at + LANES, LANES), LANES)]

        before = layer(l - 1) if l > 0 else depth_in[0, :, here] * from_prv
        after = layer(l + 1) if l < layers - 1 else depth_in[1, :, here] * from_nxt
        tiles = split(layer(l))
        left = split(x[l, :, pl.ds(at, LANES)])
        right = split(x[l, :, pl.ds(pl.multiple_of(at + 2 * LANES, LANES), LANES)])
        over_row = jnp.broadcast_to(rows_in[0, l : l + 1, here], tile) * from_up
        under_row = jnp.broadcast_to(rows_in[1, l : l + 1, here], tile) * from_down
        behind = [shifted([t], 1, e, lane, 1)[0] for t, e in zip(tiles, left)]
        ahead = [shifted([t], -1, e, lane, 1)[0] for t, e in zip(tiles, right)]
        above = shifted(tiles, 1, over_row, row, 0)
        below = shifted(tiles, -1, under_row, row, 0)
        hx, hy, hz = (wide(2 * bumps + c) for c in range(3))
        facing = (
            hx * (after - before)
            + hy * jnp.concatenate([b - a for a, b in zip(above, below)], 0)
            + hz * jnp.concatenate([b - a for a, b in zip(behind, ahead)], 0)
        )
        shading = 5.0 / 3.0 + jnp.tanh(facing)
        local = pl.ds(pl.multiple_of(i * LANES, LANES), LANES)
        seen = clear * emi[s, l, 0, :, local]
        lit = seen * shading
        return clear - seen, opaque + seen, [colour[c] + lit * emi[s, l, c + 1, :, local] for c in range(3)]

    def march_end(s, i, state):
        owned = regroup(state[2] + [state[1]], lane_all)
        for j in range(Q):
            p1s[s, j, i] = owned[j]

    zero = jnp.zeros((rows, LANES), jnp.float32)
    fresh = (jnp.ones((rows, LANES), jnp.float32), zero, [zero] * 3)

    def emit(s):
        def one(n, _):
            for l in range(layers // per):
                emit_layer(s, n * (layers // per) + l)
            return 0

        lax.fori_loop(0, per, one, 0)

    def march(s):
        def one(i, _):
            at, state = column_of(s, i), fresh
            for l in range(layers):
                state = march_layer(s, i, at, l, state)
            march_end(s, i, state)
            return 0

        lax.fori_loop(0, per, one, 0)

    def emit_and_march(e, s):
        def one(i, _):
            at, state = column_of(s, i), fresh
            for l in range(layers):
                if l % per == 0:
                    emit_layer(e, i * (layers // per) + l // per)
                state = march_layer(s, i, at, l, state)
            march_end(s, i, state)
            return 0

        lax.fori_loop(0, per, one, 0)

    emit(0)
    pl.semaphore_wait(barrier, 4 + (nz - 1) + per * (Q - 1))

    def send_depth(s):
        depth_copy(0, s, nxt // Q, nxt).start()
        depth_copy(1, s, prv // Q, prv).start()

    send_depth(0)
    for side in range(2):
        rows_copy(side).start()
    for s in range(1, LEAD):
        send_depth(s)
    for s in range(1, LEAD):
        emit(s)

    def send_more(s, _):
        send_depth(s)
        return 0

    lax.fori_loop(LEAD, PARTS, send_more, 0)
    for side in range(2):
        rows_copy(side).wait_recv()


    def step(s, _):
        @pl.when(s < PARTS)
        def _():
            for side in range(2):
                depth_copy(side, s, z, (nxt, prv)[side]).wait_recv()

        @pl.when(s + LEAD < PARTS)
        def _():
            emit_and_march(s + LEAD, s)

        @pl.when((s + LEAD >= PARTS) & (s < PARTS))
        def _():
            march(s)

        @pl.when(s < PARTS - 1)
        def _():
            for k in (2, 1, 3):
                p1_copy(s, k).start()

        @pl.when(s == PARTS - 1)
        def _():
            for g in range(per):
                for k in range(Q):
                    if (g, k) != (0, 0):
                        last_copy(g, k).start()

        @pl.when(s >= 2)
        def _():
            t = s - 2
            first = part_at(t, z) * per
            p1r[t, 0] = p1s[t, y]
            for k in range(1, Q):
                p1_copy(t, k).wait_recv()
            flat = (per * rows, LANES)
            lane_flat = lax.broadcasted_iota(jnp.int32, flat, 1)
            total = p1r[t, lax.rem(y + 1, Q)].reshape(flat)
            for j in range(Q - 2, -1, -1):
                total = over(p1r[t, lax.rem(y + Q - j, Q)].reshape(flat), total, lane_flat)
            total = total.reshape(per, rows, LANES)
            for b in range(per):
                p2s[first + b] = total[b]
                p2_copy(lax.rem(first + b + nz - z, nz)).start()

        return 0

    lax.fori_loop(0, PARTS + 1, step, 0)

    for side in range(2):
        rows_copy(side).wait_send()

    def finish(s, _):
        for side in range(2):
            depth_copy(side, s, z, (nxt, prv)[side]).wait_send()

        @pl.when(s < PARTS - 1)
        def _():
            for k in range(1, Q):
                p1_copy(s, k).wait_send()

        return 0

    lax.fori_loop(0, PARTS, finish, 0)

    lastr[0, 0] = p1s[PARTS - 1, y, in_group]
    for g in range(per):
        for k in range(Q):
            if (g, k) != (0, 0):
                last_copy(g, k).wait()
    for g in range(per):
        near = lax.rem(in_group + per - g, per)
        total = lastr[near, lax.rem(y + 1, Q)]
        for j in range(Q - 2, -1, -1):
            total = over(lastr[near, lax.rem(y + Q - j, Q)], total, lane_all)
        p2r[lax.rem(z + nz - (first_z + g), nz)] = total

    def finish_p2(i, _):
        other = lax.rem(first_z + i, nz)
        p2_copy(lax.rem(other + nz - z, nz)).wait_send()
        p2_copy(lax.rem(z + nz - other, nz)).wait_recv()
        return 0

    lax.fori_loop(per, nz, finish_p2, 0)

    total = p2r[lax.rem(z + 1, nz)]
    for i in range(1, nz):
        total = over(p2r[lax.rem(z + 1 + i, nz)], total, lane_all)
    for c in range(4):
        out[c] = total[:, G * c : G * c + G]


def local(nx, ny, density, centers, widths, weights, colors, light):
    layers, rows, cols = density.shape
    nz, bumps = nx // Q, centers.shape[0]
    width = cols // PARTS
    per = width // LANES
    dma = pltpu.SemaphoreType.DMA
    hbm = pl.BlockSpec(memory_space=pltpu.HBM)
    f32 = jnp.float32
    return pl.pallas_call(
        functools.partial(kernel, nx, ny, 1.5 / (layers * nx)),
        out_shape=jax.ShapeDtypeStruct((4, rows, cols // nx), f32),
        in_specs=[hbm] * 6,
        out_specs=pl.BlockSpec(memory_space=pltpu.VMEM),
        scratch_shapes=[pltpu.SMEM(given.shape, f32) for given in (centers, widths, weights, colors, light)]
        + [
            pltpu.VMEM((layers, rows, cols + 2 * LANES), f32),
            pltpu.VMEM((2, layers, cols), f32),
            pltpu.VMEM((2, layers, cols), f32),
            pltpu.VMEM((2, rows, cols), f32),
            pltpu.VMEM((2 * bumps + 3, 8, LANES), f32),
            pltpu.VMEM((8 * rows, DEEP), jnp.bfloat16),
            pltpu.VMEM((PARTS, layers, 4, rows, width), f32),
            pltpu.VMEM((PARTS, Q, per, rows, LANES), f32),
            pltpu.VMEM((PARTS - 1, Q, per, rows, LANES), f32),
            pltpu.VMEM((per, Q, rows, LANES), f32),
            pltpu.VMEM((nz, rows, LANES), f32),
            pltpu.VMEM((nz, rows, LANES), f32),
            dma,
            dma((5,)),
            dma((2,)),
            dma((2,)),
            dma((2, PARTS)),
            dma((2, PARTS)),
            dma((PARTS - 1, Q)),
            dma((PARTS - 1, Q)),
            dma((per, Q)),
            dma((per, Q)),
            dma((nz,)),
            dma((nz,)),
        ],
        compiler_params=pltpu.CompilerParams(
            collective_id=0, has_side_effects=True, vmem_limit_bytes=40 * 1024 * 1024
        ),
        cost_estimate=pl.CostEstimate(
            flops=130 * density.size, bytes_accessed=4 * density.size, transcendentals=9 * density.size
        ),
    )(*(pltpu.with_memory_space_constraint(v, pltpu.HBM) for v in (density, centers, widths, weights, colors, light)))


def solution(mesh):
    nx, ny = mesh.shape["gx"], mesh.shape["gy"]
    in_specs = (P("gx", "gy", None), P(), P(), P(), P(), P())
    out_specs = P(None, "gy", "gx")
    return jax.shard_map(
        functools.partial(local, nx, ny), mesh=mesh, in_specs=in_specs, out_specs=out_specs, check_vma=False
    )
```

```python
import functools
import math

import jax
import jax.numpy as jnp
from jax import lax
from jax.experimental import pallas as pl
from jax.experimental.pallas import tpu as pltpu
from jax.sharding import PartitionSpec as P

MESH = pl.DeviceIdType.MESH
LANES = 128
Q = 4
DEEP = 256
G = LANES // Q
PARTS = 8
LEAD = 3


def roll_lanes(v, by):
    return pltpu.roll(v, by % LANES, axis=1)


def shifted(tiles, by, edge, lane_or_row, axis):
    size = tiles[0].shape[axis]
    if by > 0:
        ahead, at = [edge] + tiles[:-1], size - 1
    else:
        ahead, at = tiles[1:] + [edge], 0
    return [pltpu.roll(jnp.where(lane_or_row == at, a, t), by % size, axis=axis) for a, t in zip(ahead, tiles)]


def regroup(values, lane):
    a, b, c, d = values
    low = lane < 2 * G
    ac0 = jnp.where(low, a, roll_lanes(c, 2 * G))
    ac1 = jnp.where(low, roll_lanes(a, -2 * G), c)
    bd0 = jnp.where(low, b, roll_lanes(d, 2 * G))
    bd1 = jnp.where(low, roll_lanes(b, -2 * G), d)
    even = lax.rem(lane // G, 2) == 0
    out = []
    for first, second in ((ac0, bd0), (ac1, bd1)):
        out.append(jnp.where(even, first, roll_lanes(second, G)))
        out.append(jnp.where(even, roll_lanes(first, -G), second))
    return out


def over(front, back, lane):
    clear = 1.0 - front
    ends = jnp.where(lane < G, roll_lanes(clear, G), clear)
    inner = (lane >= G) & (lane < 3 * G)
    return front + jnp.where(inner, roll_lanes(ends, 2 * G), ends) * back


def kernel(
    nx, ny, step_size, density, *rest,
):
    given, rest = rest[:5], rest[5:]
    out, centers, widths, weights, colors, light = rest[:6]
    x, rows_out, rows_in, depth_in, prm, mix, emi, p1s, p1r, lastr, p2s, p2r = rest[6:18]
    x_sem, given_sem, rows_ss, rows_rs, depth_ss, depth_rs, p1_ss, p1_rs, last_ss, last_rs, p2_ss, p2_rs = rest[18:]
    layers, rows, cols = density.shape
    nz = nx // Q
    bumps = centers.shape[0]
    width = cols // PARTS
    per = width // LANES
    me, my = lax.axis_index("gx"), lax.axis_index("gy")
    z, y = me // Q, lax.rem(me, Q)
    first_z, in_group = z // per * per, lax.rem(z, per)
    nxt, prv = lax.rem(me + 1, nx), lax.rem(me + nx - 1, nx)
    down, up = lax.rem(my + 1, ny), lax.rem(my + ny - 1, ny)

    load = pltpu.make_async_copy(density, x.at[:, :, pl.ds(LANES, cols)], x_sem)
    load.start()
    fetches = [
        pltpu.make_async_copy(src, dst, given_sem.at[i])
        for i, (src, dst) in enumerate(zip(given, (centers, widths, weights, colors, light)))
    ]
    for fetch in fetches:
        fetch.start()

    barrier = pltpu.get_barrier_semaphore()

    def greet(gx, gy):
        pl.semaphore_signal(barrier, inc=1, device_id=(gx, gy), device_id_type=MESH)

    greet(nxt, my)
    greet(prv, my)
    greet(me, down)
    greet(me, up)

    def greet_z(k, _):
        greet(lax.rem(z + k, nz) * Q + y, my)
        return 0

    lax.fori_loop(1, nz, greet_z, 0)
    for k in range(1, Q):
        for g in range(per):
            greet((first_z + lax.rem(in_group + g, per)) * Q + lax.rem(y + k, Q), my)
    x[:, :, :LANES] = jnp.zeros((layers, rows, LANES), jnp.float32)
    x[:, :, LANES + cols :] = jnp.zeros((layers, rows, LANES), jnp.float32)

    def part_at(s, place):
        away = jnp.where(lax.rem(s, 2) == 0, s // 2, PARTS - (s + 1) // 2)
        return lax.rem(place // per + PARTS // 2 + away, PARTS)

    def rows_copy(side):
        return pltpu.make_async_remote_copy(
            src_ref=rows_out.at[1 - side],
            dst_ref=rows_in.at[side],
            send_sem=rows_ss.at[side],
            recv_sem=rows_rs.at[side],
            device_id=(me, down if side == 0 else up),
            device_id_type=MESH,
        )

    def depth_copy(side, s, place, gx):
        start = pl.multiple_of(part_at(s, place) * width, width)
        return pltpu.make_async_remote_copy(
            src_ref=density.at[layers - 1 if side == 0 else 0, :, pl.ds(start, width)],
            dst_ref=depth_in.at[side, :, pl.ds(start, width)],
            send_sem=depth_ss.at[side, s],
            recv_sem=depth_rs.at[side, s],
            device_id=(gx, my),
            device_id_type=MESH,
        )

    def p1_copy(s, k):
        to = lax.rem(y + k, Q)
        return pltpu.make_async_remote_copy(
            src_ref=p1s.at[s, to],
            dst_ref=p1r.at[s, k],
            send_sem=p1_ss.at[s, k],
            recv_sem=p1_rs.at[s, k],
            device_id=(z * Q + to, my),
            device_id_type=MESH,
        )

    def last_copy(g, k):
        at, to = lax.rem(in_group + g, per), lax.rem(y + k, Q)
        return pltpu.make_async_remote_copy(
            src_ref=p1s.at[PARTS - 1, to, at],
            dst_ref=lastr.at[g, k],
            send_sem=last_ss.at[g, k],
            recv_sem=last_rs.at[g, k],
            device_id=((first_z + at) * Q + to, my),
            device_id_type=MESH,
        )

    def p2_copy(k):
        to = lax.rem(z + k, nz)
        return pltpu.make_async_remote_copy(
            src_ref=p2s.at[to],
            dst_ref=p2r.at[k],
            send_sem=p2_ss.at[k],
            recv_sem=p2_rs.at[k],
            device_id=(to * Q + y, my),
            device_id_type=MESH,
        )

    for fetch in fetches:
        fetch.wait()
    tile = (8, LANES)
    scale = math.sqrt(math.log2(math.e))
    for k in range(bumps):
        inverse = scale / jnp.full(tile, widths[k], jnp.float32)
        prm[2 * k] = jnp.full(tile, centers[k], jnp.float32)
        prm[2 * k + 1] = -inverse * inverse
    for c in range(3):
        prm[2 * bumps + c] = jnp.full(tile, 0.5 * light[c], jnp.float32)
    into = lax.broadcasted_iota(jnp.int32, (rows, DEEP), 0)
    out_of = lax.broadcasted_iota(jnp.int32, (rows, DEEP), 1)
    lines = []
    for c in range(4):
        line = jnp.zeros((rows, DEEP), jnp.float32)
        for k in range(bumps):
            factor = weights[k] * step_size if c == 0 else colors[c - 1, k] * 0.375
            line = jnp.where(out_of == into + k * rows, factor, line)
        lines.append(line)
    exact = jnp.concatenate(lines, 0)
    high = exact.astype(jnp.bfloat16)
    mix[: 4 * rows] = high
    mix[4 * rows :] = (exact - high.astype(jnp.float32)).astype(jnp.bfloat16)

    load.wait()
    for l in range(layers):
        rows_out[0, l : l + 1, :] = x[l, 0:1, LANES : LANES + cols]
        rows_out[1, l : l + 1, :] = x[l, rows - 1 : rows, LANES : LANES + cols]

    lane = lax.broadcasted_iota(jnp.int32, tile, 1)
    row = lax.broadcasted_iota(jnp.int32, tile, 0)
    lane_all = lax.broadcasted_iota(jnp.int32, (rows, LANES), 1)
    from_prv = jnp.where(me > 0, 1.0, 0.0).astype(jnp.float32)
    from_nxt = jnp.where(me < nx - 1, 1.0, 0.0).astype(jnp.float32)
    from_up = jnp.where(my > 0, 1.0, 0.0).astype(jnp.float32)
    from_down = jnp.where(my < ny - 1, 1.0, 0.0).astype(jnp.float32)
    n_row = rows // 8

    def wide(i):
        return jnp.concatenate([prm[i]] * n_row, 0)

    def split(v):
        return [v[8 * r : 8 * r + 8] for r in range(n_row)]

    def column_of(s, i):
        return pl.multiple_of(part_at(s, z) * width + i * LANES, LANES)

    def broad(i):
        return jnp.concatenate([wide(i)] * per, 1)

    def emit_layer(s, l):
        cells = x[l, :, pl.ds(pl.multiple_of(part_at(s, z) * width + LANES, LANES), width)]
        stack = []
        for k in range(bumps):
            away = cells - broad(2 * k)
            stack.append(jnp.exp2(away * away * broad(2 * k + 1)))
        if DEEP > bumps * rows:
            stack.append(jnp.zeros((DEEP - bumps * rows, width), jnp.float32))
        exact = jnp.concatenate(stack, 0)
        high = exact.astype(jnp.bfloat16)
        low = (exact - high.astype(jnp.float32)).astype(jnp.bfloat16)
        most = jnp.dot(mix[...], high, preferred_element_type=jnp.float32)
        rest = jnp.dot(mix[: 4 * rows], low, preferred_element_type=jnp.float32)
        sums = most[: 4 * rows] + (most[4 * rows :] + rest)
        t = sums[:rows]
        opacity = t * (1.0 - t * (0.5 - t * (1.0 / 6.0 - t * (1.0 / 24.0))))
        emi[s, l, 0] = opacity
        for c in range(1, 4):
            emi[s, l, c] = sums[c * rows : (c + 1) * rows]

    def march_layer(s, i, at, l, state):
        clear, opaque, colour = state
        here = pl.ds(at, LANES)

        def layer(n):
            return x[n, :, pl.ds(pl.multiple_of(at + LANES, LANES), LANES)]

        before = layer(l - 1) if l > 0 else depth_in[0, :, here] * from_prv
        after = layer(l + 1) if l < layers - 1 else depth_in[1, :, here] * from_nxt
        tiles = split(layer(l))
        left = split(x[l, :, pl.ds(at, LANES)])
        right = split(x[l, :, pl.ds(pl.multiple_of(at + 2 * LANES, LANES), LANES)])
        over_row = jnp.broadcast_to(rows_in[0, l : l + 1, here], tile) * from_up
        under_row = jnp.broadcast_to(rows_in[1, l : l + 1, here], tile) * from_down
        behind = [shifted([t], 1, e, lane, 1)[0] for t, e in zip(tiles, left)]
        ahead = [shifted([t], -1, e, lane, 1)[0] for t, e in zip(tiles, right)]
        above = shifted(tiles, 1, over_row, row, 0)
        below = shifted(tiles, -1, under_row, row, 0)
        hx, hy, hz = (wide(2 * bumps + c) for c in range(3))
        facing = (
            hx * (after - before)
            + hy * jnp.concatenate([b - a for a, b in zip(above, below)], 0)
            + hz * jnp.concatenate([b - a for a, b in zip(behind, ahead)], 0)
        )
        shading = 5.0 / 3.0 + jnp.tanh(facing)
        local = pl.ds(pl.multiple_of(i * LANES, LANES), LANES)
        seen = clear * emi[s, l, 0, :, local]
        lit = seen * shading
        return clear - seen, opaque + seen, [colour[c] + lit * emi[s, l, c + 1, :, local] for c in range(3)]

    def march_end(s, i, state):
        owned = regroup(state[2] + [state[1]], lane_all)
        for j in range(Q):
            p1s[s, j, i] = owned[j]

    zero = jnp.zeros((rows, LANES), jnp.float32)
    fresh = (jnp.ones((rows, LANES), jnp.float32), zero, [zero] * 3)

    def emit(s):
        def one(n, _):
            for l in range(layers // per):
                emit_layer(s, n * (layers // per) + l)
            return 0

        lax.fori_loop(0, per, one, 0)

    def march(s):
        def one(i, _):
            at, state = column_of(s, i), fresh
            for l in range(layers):
                state = march_layer(s, i, at, l, state)
            march_end(s, i, state)
            return 0

        lax.fori_loop(0, per, one, 0)

    def emit_and_march(e, s):
        def one(i, _):
            at, state = column_of(s, i), fresh
            for l in range(layers):
                if l % per == 0:
                    emit_layer(e, i * (layers // per) + l // per)
                state = march_layer(s, i, at, l, state)
            march_end(s, i, state)
            return 0

        lax.fori_loop(0, per, one, 0)

    emit(0)
    pl.semaphore_wait(barrier, 4 + (nz - 1) + per * (Q - 1))

    def send_depth(s):
        depth_copy(0, s, nxt // Q, nxt).start()
        depth_copy(1, s, prv // Q, prv).start()

    send_depth(0)
    for side in range(2):
        rows_copy(side).start()
    for s in range(1, LEAD):
        send_depth(s)
    for s in range(1, LEAD):
        emit(s)

    def send_more(s, _):
        send_depth(s)
        return 0

    lax.fori_loop(LEAD, PARTS, send_more, 0)
    for side in range(2):
        rows_copy(side).wait_recv()


    last = PARTS - 1

    def halos_in(s):
        for side in range(2):
            depth_copy(side, s, z, (nxt, prv)[side]).wait_recv()

    def step(s, _):
        @pl.when(s < last)
        def _():
            halos_in(s)

            @pl.when(s + LEAD < last)
            def _():
                emit_and_march(s + LEAD, s)

            @pl.when(s + LEAD >= last)
            def _():
                march(s)

            for k in (2, 1, 3):
                p1_copy(s, k).start()

        @pl.when(s == last)
        def _():
            emit(last)

        @pl.when(s == last + 1)
        def _():
            halos_in(last)
            march(last)
            for g in range(per):
                for k in range(Q):
                    if (g, k) != (0, 0):
                        last_copy(g, k).start()

        @pl.when((s == LEAD) | (s >= last - 1))
        def _():
            t = jnp.where(s == LEAD, 0, s - (last - 2))
            first = part_at(t, z) * per
            p1r[t, 0] = p1s[t, y]
            for k in range(1, Q):
                p1_copy(t, k).wait_recv()
            flat = (per * rows, LANES)
            lane_flat = lax.broadcasted_iota(jnp.int32, flat, 1)
            total = p1r[t, lax.rem(y + 1, Q)].reshape(flat)
            for j in range(Q - 2, -1, -1):
                total = over(p1r[t, lax.rem(y + Q - j, Q)].reshape(flat), total, lane_flat)
            total = total.reshape(per, rows, LANES)
            for b in range(per):
                p2s[first + b] = total[b]
                p2_copy(lax.rem(first + b + nz - z, nz)).start()

        return 0

    lax.fori_loop(0, 2 * last - 2, step, 0)

    for side in range(2):
        rows_copy(side).wait_send()

    def finish(s, _):
        for side in range(2):
            depth_copy(side, s, z, (nxt, prv)[side]).wait_send()

        @pl.when(s < PARTS - 1)
        def _():
            for k in range(1, Q):
                p1_copy(s, k).wait_send()

        return 0

    lax.fori_loop(0, PARTS, finish, 0)

    lastr[0, 0] = p1s[PARTS - 1, y, in_group]
    for g in range(per):
        for k in range(Q):
            if (g, k) != (0, 0):
                last_copy(g, k).wait()
    for g in range(per):
        near = lax.rem(in_group + per - g, per)
        total = lastr[near, lax.rem(y + 1, Q)]
        for j in range(Q - 2, -1, -1):
            total = over(lastr[near, lax.rem(y + Q - j, Q)], total, lane_all)
        p2r[lax.rem(z + nz - (first_z + g), nz)] = total

    def finish_p2(i, _):
        other = lax.rem(first_z + i, nz)
        p2_copy(lax.rem(other + nz - z, nz)).wait_send()
        p2_copy(lax.rem(z + nz - other, nz)).wait_recv()
        return 0

    lax.fori_loop(per, nz, finish_p2, 0)

    total = p2r[lax.rem(z + 1, nz)]
    for i in range(1, nz):
        total = over(p2r[lax.rem(z + 1 + i, nz)], total, lane_all)
    for c in range(4):
        out[c] = total[:, G * c : G * c + G]


def local(nx, ny, density, centers, widths, weights, colors, light):
    layers, rows, cols = density.shape
    nz, bumps = nx // Q, centers.shape[0]
    width = cols // PARTS
    per = width // LANES
    dma = pltpu.SemaphoreType.DMA
    hbm = pl.BlockSpec(memory_space=pltpu.HBM)
    f32 = jnp.float32
    return pl.pallas_call(
        functools.partial(kernel, nx, ny, 1.5 / (layers * nx)),
        out_shape=jax.ShapeDtypeStruct((4, rows, cols // nx), f32),
        in_specs=[hbm] * 6,
        out_specs=pl.BlockSpec(memory_space=pltpu.VMEM),
        scratch_shapes=[pltpu.SMEM(given.shape, f32) for given in (centers, widths, weights, colors, light)]
        + [
            pltpu.VMEM((layers, rows, cols + 2 * LANES), f32),
            pltpu.VMEM((2, layers, cols), f32),
            pltpu.VMEM((2, layers, cols), f32),
            pltpu.VMEM((2, rows, cols), f32),
            pltpu.VMEM((2 * bumps + 3, 8, LANES), f32),
            pltpu.VMEM((8 * rows, DEEP), jnp.bfloat16),
            pltpu.VMEM((PARTS, layers, 4, rows, width), f32),
            pltpu.VMEM((PARTS, Q, per, rows, LANES), f32),
            pltpu.VMEM((PARTS - 1, Q, per, rows, LANES), f32),
            pltpu.VMEM((per, Q, rows, LANES), f32),
            pltpu.VMEM((nz, rows, LANES), f32),
            pltpu.VMEM((nz, rows, LANES), f32),
            dma,
            dma((5,)),
            dma((2,)),
            dma((2,)),
            dma((2, PARTS)),
            dma((2, PARTS)),
            dma((PARTS - 1, Q)),
            dma((PARTS - 1, Q)),
            dma((per, Q)),
            dma((per, Q)),
            dma((nz,)),
            dma((nz,)),
        ],
        compiler_params=pltpu.CompilerParams(
            collective_id=0, has_side_effects=True, vmem_limit_bytes=40 * 1024 * 1024
        ),
        cost_estimate=pl.CostEstimate(
            flops=130 * density.size, bytes_accessed=4 * density.size, transcendentals=9 * density.size
        ),
    )(*(pltpu.with_memory_space_constraint(v, pltpu.HBM) for v in (density, centers, widths, weights, colors, light)))


def solution(mesh):
    nx, ny = mesh.shape["gx"], mesh.shape["gy"]
    in_specs = (P("gx", "gy", None), P(), P(), P(), P(), P())
    out_specs = P(None, "gy", "gx")
    return jax.shard_map(
        functools.partial(local, nx, ny), mesh=mesh, in_specs=in_specs, out_specs=out_specs, check_vma=False
    )
```

```python
import functools
import math

import jax
import jax.numpy as jnp
from jax import lax
from jax.experimental import pallas as pl
from jax.experimental.pallas import tpu as pltpu
from jax.sharding import PartitionSpec as P

MESH = pl.DeviceIdType.MESH
LANES = 128
Q = 4
DEEP = 256
G = LANES // Q
PARTS = 8
LEAD = 3


def roll_lanes(v, by):
    return pltpu.roll(v, by % LANES, axis=1)


def shifted(tiles, by, edge, lane_or_row, axis):
    size = tiles[0].shape[axis]
    if by > 0:
        ahead, at = [edge] + tiles[:-1], size - 1
    else:
        ahead, at = tiles[1:] + [edge], 0
    return [pltpu.roll(jnp.where(lane_or_row == at, a, t), by % size, axis=axis) for a, t in zip(ahead, tiles)]


def regroup(values, lane):
    a, b, c, d = values
    low = lane < 2 * G
    ac0 = jnp.where(low, a, roll_lanes(c, 2 * G))
    ac1 = jnp.where(low, roll_lanes(a, -2 * G), c)
    bd0 = jnp.where(low, b, roll_lanes(d, 2 * G))
    bd1 = jnp.where(low, roll_lanes(b, -2 * G), d)
    even = lax.rem(lane // G, 2) == 0
    out = []
    for first, second in ((ac0, bd0), (ac1, bd1)):
        out.append(jnp.where(even, first, roll_lanes(second, G)))
        out.append(jnp.where(even, roll_lanes(first, -G), second))
    return out


def over(front, back, lane):
    clear = 1.0 - front
    ends = jnp.where(lane < G, roll_lanes(clear, G), clear)
    inner = (lane >= G) & (lane < 3 * G)
    return front + jnp.where(inner, roll_lanes(ends, 2 * G), ends) * back


def kernel(
    nx, ny, step_size, density, *rest,
):
    given, rest = rest[:5], rest[5:]
    out, centers, widths, weights, colors, light = rest[:6]
    x, rows_out, rows_in, depth_in, prm, mix, emi, p1s, p1r, lastr, p2s, p2r = rest[6:18]
    x_sem, given_sem, rows_ss, rows_rs, depth_ss, depth_rs, p1_ss, p1_rs, last_ss, last_rs, p2_ss, p2_rs = rest[18:]
    layers, rows, cols = density.shape
    nz = nx // Q
    bumps = centers.shape[0]
    width = cols // PARTS
    per = width // LANES
    me, my = lax.axis_index("gx"), lax.axis_index("gy")
    z, y = me // Q, lax.rem(me, Q)
    first_z, in_group = z // per * per, lax.rem(z, per)
    nxt, prv = lax.rem(me + 1, nx), lax.rem(me + nx - 1, nx)
    down, up = lax.rem(my + 1, ny), lax.rem(my + ny - 1, ny)

    load = pltpu.make_async_copy(density, x.at[:, :, pl.ds(LANES, cols)], x_sem)
    load.start()
    fetches = [
        pltpu.make_async_copy(src, dst, given_sem.at[i])
        for i, (src, dst) in enumerate(zip(given, (centers, widths, weights, colors, light)))
    ]
    for fetch in fetches:
        fetch.start()

    barrier = pltpu.get_barrier_semaphore()

    def greet(gx, gy):
        pl.semaphore_signal(barrier, inc=1, device_id=(gx, gy), device_id_type=MESH)

    greet(nxt, my)
    greet(prv, my)
    greet(me, down)
    greet(me, up)

    def greet_z(k, _):
        greet(lax.rem(z + k, nz) * Q + y, my)
        return 0

    lax.fori_loop(1, nz, greet_z, 0)
    for k in range(1, Q):
        for g in range(per):
            greet((first_z + lax.rem(in_group + g, per)) * Q + lax.rem(y + k, Q), my)
    x[:, :, :LANES] = jnp.zeros((layers, rows, LANES), jnp.float32)
    x[:, :, LANES + cols :] = jnp.zeros((layers, rows, LANES), jnp.float32)

    def part_at(s, place):
        away = jnp.where(lax.rem(s, 2) == 0, s // 2, PARTS - (s + 1) // 2)
        return lax.rem(place // per + PARTS // 2 + away, PARTS)

    def rows_copy(side):
        return pltpu.make_async_remote_copy(
            src_ref=rows_out.at[1 - side],
            dst_ref=rows_in.at[side],
            send_sem=rows_ss.at[side],
            recv_sem=rows_rs.at[side],
            device_id=(me, down if side == 0 else up),
            device_id_type=MESH,
        )

    def depth_copy(side, s, place, gx):
        start = pl.multiple_of(part_at(s, place) * width, width)
        return pltpu.make_async_remote_copy(
            src_ref=density.at[layers - 1 if side == 0 else 0, :, pl.ds(start, width)],
            dst_ref=depth_in.at[side, :, pl.ds(start, width)],
            send_sem=depth_ss.at[side, s],
            recv_sem=depth_rs.at[side, s],
            device_id=(gx, my),
            device_id_type=MESH,
        )

    def p1_copy(s, k):
        to = lax.rem(y + k, Q)
        return pltpu.make_async_remote_copy(
            src_ref=p1s.at[s, to],
            dst_ref=p1r.at[s, k],
            send_sem=p1_ss.at[s, k],
            recv_sem=p1_rs.at[s, k],
            device_id=(z * Q + to, my),
            device_id_type=MESH,
        )

    def last_copy(g, k):
        at, to = lax.rem(in_group + g, per), lax.rem(y + k, Q)
        return pltpu.make_async_remote_copy(
            src_ref=p1s.at[PARTS - 1, to, at],
            dst_ref=lastr.at[g, k],
            send_sem=last_ss.at[g, k],
            recv_sem=last_rs.at[g, k],
            device_id=((first_z + at) * Q + to, my),
            device_id_type=MESH,
        )

    def p2_copy(k):
        to = lax.rem(z + k, nz)
        return pltpu.make_async_remote_copy(
            src_ref=p2s.at[to],
            dst_ref=p2r.at[k],
            send_sem=p2_ss.at[k],
            recv_sem=p2_rs.at[k],
            device_id=(to * Q + y, my),
            device_id_type=MESH,
        )

    pl.semaphore_wait(barrier, 4 + (nz - 1) + per * (Q - 1))

    def send_depth(s, _):
        depth_copy(0, s, nxt // Q, nxt).start()
        depth_copy(1, s, prv // Q, prv).start()
        return 0

    lax.fori_loop(0, PARTS, send_depth, 0)

    for fetch in fetches:
        fetch.wait()
    tile = (8, LANES)
    scale = math.sqrt(math.log2(math.e))
    for k in range(bumps):
        inverse = scale / jnp.full(tile, widths[k], jnp.float32)
        prm[2 * k] = jnp.full(tile, centers[k], jnp.float32)
        prm[2 * k + 1] = -inverse * inverse
    for c in range(3):
        prm[2 * bumps + c] = jnp.full(tile, 0.5 * light[c], jnp.float32)
    into = lax.broadcasted_iota(jnp.int32, (rows, DEEP), 0)
    out_of = lax.broadcasted_iota(jnp.int32, (rows, DEEP), 1)
    lines = []
    for c in range(4):
        line = jnp.zeros((rows, DEEP), jnp.float32)
        for k in range(bumps):
            factor = weights[k] * step_size if c == 0 else colors[c - 1, k] * 0.375
            line = jnp.where(out_of == into + k * rows, factor, line)
        lines.append(line)
    exact = jnp.concatenate(lines, 0)
    high = exact.astype(jnp.bfloat16)
    mix[: 4 * rows] = high
    mix[4 * rows :] = (exact - high.astype(jnp.float32)).astype(jnp.bfloat16)

    load.wait()
    for l in range(layers):
        rows_out[0, l : l + 1, :] = x[l, 0:1, LANES : LANES + cols]
        rows_out[1, l : l + 1, :] = x[l, rows - 1 : rows, LANES : LANES + cols]
    for side in range(2):
        rows_copy(side).start()

    lane = lax.broadcasted_iota(jnp.int32, tile, 1)
    row = lax.broadcasted_iota(jnp.int32, tile, 0)
    lane_all = lax.broadcasted_iota(jnp.int32, (rows, LANES), 1)
    from_prv = jnp.where(me > 0, 1.0, 0.0).astype(jnp.float32)
    from_nxt = jnp.where(me < nx - 1, 1.0, 0.0).astype(jnp.float32)
    from_up = jnp.where(my > 0, 1.0, 0.0).astype(jnp.float32)
    from_down = jnp.where(my < ny - 1, 1.0, 0.0).astype(jnp.float32)
    n_row = rows // 8

    def wide(i):
        return jnp.concatenate([prm[i]] * n_row, 0)

    def split(v):
        return [v[8 * r : 8 * r + 8] for r in range(n_row)]

    def column_of(s, i):
        return pl.multiple_of(part_at(s, z) * width + i * LANES, LANES)

    def broad(i):
        return jnp.concatenate([wide(i)] * per, 1)

    def emit_layer(s, l):
        cells = x[l, :, pl.ds(pl.multiple_of(part_at(s, z) * width + LANES, LANES), width)]
        stack = []
        for k in range(bumps):
            away = cells - broad(2 * k)
            stack.append(jnp.exp2(away * away * broad(2 * k + 1)))
        if DEEP > bumps * rows:
            stack.append(jnp.zeros((DEEP - bumps * rows, width), jnp.float32))
        exact = jnp.concatenate(stack, 0)
        high = exact.astype(jnp.bfloat16)
        low = (exact - high.astype(jnp.float32)).astype(jnp.bfloat16)
        most = jnp.dot(mix[...], high, preferred_element_type=jnp.float32)
        rest = jnp.dot(mix[: 4 * rows], low, preferred_element_type=jnp.float32)
        sums = most[: 4 * rows] + (most[4 * rows :] + rest)
        t = sums[:rows]
        opacity = t * (1.0 - t * (0.5 - t * (1.0 / 6.0 - t * (1.0 / 24.0))))
        emi[s, l, 0] = opacity
        for c in range(1, 4):
            emi[s, l, c] = sums[c * rows : (c + 1) * rows]

    def march_layer(s, i, at, l, state):
        clear, opaque, colour = state
        here = pl.ds(at, LANES)

        def layer(n):
            return x[n, :, pl.ds(pl.multiple_of(at + LANES, LANES), LANES)]

        before = layer(l - 1) if l > 0 else depth_in[0, :, here] * from_prv
        after = layer(l + 1) if l < layers - 1 else depth_in[1, :, here] * from_nxt
        tiles = split(layer(l))
        left = split(x[l, :, pl.ds(at, LANES)])
        right = split(x[l, :, pl.ds(pl.multiple_of(at + 2 * LANES, LANES), LANES)])
        over_row = jnp.broadcast_to(rows_in[0, l : l + 1, here], tile) * from_up
        under_row = jnp.broadcast_to(rows_in[1, l : l + 1, here], tile) * from_down
        behind = [shifted([t], 1, e, lane, 1)[0] for t, e in zip(tiles, left)]
        ahead = [shifted([t], -1, e, lane, 1)[0] for t, e in zip(tiles, right)]
        above = shifted(tiles, 1, over_row, row, 0)
        below = shifted(tiles, -1, under_row, row, 0)
        hx, hy, hz = (wide(2 * bumps + c) for c in range(3))
        facing = (
            hx * (after - before)
            + hy * jnp.concatenate([b - a for a, b in zip(above, below)], 0)
            + hz * jnp.concatenate([b - a for a, b in zip(behind, ahead)], 0)
        )
        shading = 5.0 / 3.0 + jnp.tanh(facing)
        local = pl.ds(pl.multiple_of(i * LANES, LANES), LANES)
        seen = clear * emi[s, l, 0, :, local]
        lit = seen * shading
        return clear - seen, opaque + seen, [colour[c] + lit * emi[s, l, c + 1, :, local] for c in range(3)]

    def march_end(s, i, state):
        owned = regroup(state[2] + [state[1]], lane_all)
        for j in range(Q):
            p1s[s, j, i] = owned[j]

    zero = jnp.zeros((rows, LANES), jnp.float32)
    fresh = (jnp.ones((rows, LANES), jnp.float32), zero, [zero] * 3)

    def emit(s):
        def one(n, _):
            for l in range(layers // per):
                emit_layer(s, n * (layers // per) + l)
            return 0

        lax.fori_loop(0, per, one, 0)

    def march(s):
        def one(i, _):
            at, state = column_of(s, i), fresh
            for l in range(layers):
                state = march_layer(s, i, at, l, state)
            march_end(s, i, state)
            return 0

        lax.fori_loop(0, per, one, 0)

    def emit_and_march(e, s):
        def one(i, _):
            at, state = column_of(s, i), fresh
            for l in range(layers):
                if l % per == 0:
                    emit_layer(e, i * (layers // per) + l // per)
                state = march_layer(s, i, at, l, state)
            march_end(s, i, state)
            return 0

        lax.fori_loop(0, per, one, 0)


    for s in range(LEAD):
        emit(s)
    for side in range(2):
        rows_copy(side).wait_recv()


    last = PARTS - 1

    def halos_in(s):
        for side in range(2):
            depth_copy(side, s, z, (nxt, prv)[side]).wait_recv()

    def step(s, _):
        @pl.when(s < last)
        def _():
            halos_in(s)

            @pl.when(s + LEAD < last)
            def _():
                emit_and_march(s + LEAD, s)

            @pl.when(s + LEAD >= last)
            def _():
                march(s)

            for k in (2, 1, 3):
                p1_copy(s, k).start()

        @pl.when(s == last)
        def _():
            emit(last)

        @pl.when(s == last + 1)
        def _():
            halos_in(last)
            march(last)
            for g in range(per):
                for k in range(Q):
                    if (g, k) != (0, 0):
                        last_copy(g, k).start()

        @pl.when((s == LEAD) | (s >= last - 1))
        def _():
            t = jnp.where(s == LEAD, 0, s - (last - 2))
            first = part_at(t, z) * per
            p1r[t, 0] = p1s[t, y]
            for k in range(1, Q):
                p1_copy(t, k).wait_recv()
            flat = (per * rows, LANES)
            lane_flat = lax.broadcasted_iota(jnp.int32, flat, 1)
            total = p1r[t, lax.rem(y + 1, Q)].reshape(flat)
            for j in range(Q - 2, -1, -1):
                total = over(p1r[t, lax.rem(y + Q - j, Q)].reshape(flat), total, lane_flat)
            total = total.reshape(per, rows, LANES)
            for b in range(per):
                p2s[first + b] = total[b]
                p2_copy(lax.rem(first + b + nz - z, nz)).start()

        return 0

    lax.fori_loop(0, 2 * last - 2, step, 0)

    for side in range(2):
        rows_copy(side).wait_send()

    def finish(s, _):
        for side in range(2):
            depth_copy(side, s, z, (nxt, prv)[side]).wait_send()

        @pl.when(s < PARTS - 1)
        def _():
            for k in range(1, Q):
                p1_copy(s, k).wait_send()

        return 0

    lax.fori_loop(0, PARTS, finish, 0)

    lastr[0, 0] = p1s[PARTS - 1, y, in_group]
    for g in range(per):
        for k in range(Q):
            if (g, k) != (0, 0):
                last_copy(g, k).wait()
    for g in range(per):
        near = lax.rem(in_group + per - g, per)
        total = lastr[near, lax.rem(y + 1, Q)]
        for j in range(Q - 2, -1, -1):
            total = over(lastr[near, lax.rem(y + Q - j, Q)], total, lane_all)
        p2r[lax.rem(z + nz - (first_z + g), nz)] = total

    def finish_p2(i, _):
        other = lax.rem(first_z + i, nz)
        p2_copy(lax.rem(other + nz - z, nz)).wait_send()
        p2_copy(lax.rem(z + nz - other, nz)).wait_recv()
        return 0

    lax.fori_loop(per, nz, finish_p2, 0)

    total = p2r[lax.rem(z + 1, nz)]
    for i in range(1, nz):
        total = over(p2r[lax.rem(z + 1 + i, nz)], total, lane_all)
    for c in range(4):
        out[c] = total[:, G * c : G * c + G]


def local(nx, ny, density, centers, widths, weights, colors, light):
    layers, rows, cols = density.shape
    nz, bumps = nx // Q, centers.shape[0]
    width = cols // PARTS
    per = width // LANES
    dma = pltpu.SemaphoreType.DMA
    hbm = pl.BlockSpec(memory_space=pltpu.HBM)
    f32 = jnp.float32
    return pl.pallas_call(
        functools.partial(kernel, nx, ny, 1.5 / (layers * nx)),
        out_shape=jax.ShapeDtypeStruct((4, rows, cols // nx), f32),
        in_specs=[hbm] * 6,
        out_specs=pl.BlockSpec(memory_space=pltpu.VMEM),
        scratch_shapes=[pltpu.SMEM(given.shape, f32) for given in (centers, widths, weights, colors, light)]
        + [
            pltpu.VMEM((layers, rows, cols + 2 * LANES), f32),
            pltpu.VMEM((2, layers, cols), f32),
            pltpu.VMEM((2, layers, cols), f32),
            pltpu.VMEM((2, rows, cols), f32),
            pltpu.VMEM((2 * bumps + 3, 8, LANES), f32),
            pltpu.VMEM((8 * rows, DEEP), jnp.bfloat16),
            pltpu.VMEM((PARTS, layers, 4, rows, width), f32),
            pltpu.VMEM((PARTS, Q, per, rows, LANES), f32),
            pltpu.VMEM((PARTS - 1, Q, per, rows, LANES), f32),
            pltpu.VMEM((per, Q, rows, LANES), f32),
            pltpu.VMEM((nz, rows, LANES), f32),
            pltpu.VMEM((nz, rows, LANES), f32),
            dma,
            dma((5,)),
            dma((2,)),
            dma((2,)),
            dma((2, PARTS)),
            dma((2, PARTS)),
            dma((PARTS - 1, Q)),
            dma((PARTS - 1, Q)),
            dma((per, Q)),
            dma((per, Q)),
            dma((nz,)),
            dma((nz,)),
        ],
        compiler_params=pltpu.CompilerParams(
            collective_id=0, has_side_effects=True, vmem_limit_bytes=40 * 1024 * 1024
        ),
        cost_estimate=pl.CostEstimate(
            flops=130 * density.size, bytes_accessed=4 * density.size, transcendentals=9 * density.size
        ),
    )(*(pltpu.with_memory_space_constraint(v, pltpu.HBM) for v in (density, centers, widths, weights, colors, light)))


def solution(mesh):
    nx, ny = mesh.shape["gx"], mesh.shape["gy"]
    in_specs = (P("gx", "gy", None), P(), P(), P(), P(), P())
    out_specs = P(None, "gy", "gx")
    return jax.shard_map(
        functools.partial(local, nx, ny), mesh=mesh, in_specs=in_specs, out_specs=out_specs, check_vma=False
    )
```

```python
import functools
import math

import jax
import jax.numpy as jnp
from jax import lax
from jax.experimental import pallas as pl
from jax.experimental.pallas import tpu as pltpu
from jax.sharding import PartitionSpec as P

MESH = pl.DeviceIdType.MESH
LANES = 128
Q = 4
STRAIGHT = 3
DEEP = 256
G = LANES // Q
PARTS = 8
LEAD = 2


def roll_lanes(v, by):
    return pltpu.roll(v, by % LANES, axis=1)


def shifted(tiles, by, edge, lane_or_row, axis):
    size = tiles[0].shape[axis]
    if by > 0:
        ahead, at = [edge] + tiles[:-1], size - 1
    else:
        ahead, at = tiles[1:] + [edge], 0
    return [pltpu.roll(jnp.where(lane_or_row == at, a, t), by % size, axis=axis) for a, t in zip(ahead, tiles)]


def regroup(values, lane):
    a, b, c, d = values
    low = lane < 2 * G
    ac0 = jnp.where(low, a, roll_lanes(c, 2 * G))
    ac1 = jnp.where(low, roll_lanes(a, -2 * G), c)
    bd0 = jnp.where(low, b, roll_lanes(d, 2 * G))
    bd1 = jnp.where(low, roll_lanes(b, -2 * G), d)
    even = lax.rem(lane // G, 2) == 0
    out = []
    for first, second in ((ac0, bd0), (ac1, bd1)):
        out.append(jnp.where(even, first, roll_lanes(second, G)))
        out.append(jnp.where(even, roll_lanes(first, -G), second))
    return out


def over(front, back, lane):
    clear = 1.0 - front
    ends = jnp.where(lane < G, roll_lanes(clear, G), clear)
    inner = (lane >= G) & (lane < 3 * G)
    return front + jnp.where(inner, roll_lanes(ends, 2 * G), ends) * back


def kernel(
    nx, ny, step_size, density, *rest,
):
    given, rest = rest[:5], rest[5:]
    out, centers, widths, weights, colors, light = rest[:6]
    x, rows_out, rows_in, depth_in, prm, mix, emi, p1s, p1r, lastr, p2s, p2r = rest[6:18]
    x_sem, given_sem, rows_ss, rows_rs, depth_ss, depth_rs, p1_ss, p1_rs, last_ss, last_rs, p2_ss, p2_rs = rest[18:]
    layers, rows, cols = density.shape
    nz = nx // Q
    bumps = centers.shape[0]
    width = cols // PARTS
    per = width // LANES
    me, my = lax.axis_index("gx"), lax.axis_index("gy")
    z, y = me // Q, lax.rem(me, Q)
    first_z, in_group = z // per * per, lax.rem(z, per)
    nxt, prv = lax.rem(me + 1, nx), lax.rem(me + nx - 1, nx)
    down, up = lax.rem(my + 1, ny), lax.rem(my + ny - 1, ny)

    load = pltpu.make_async_copy(density, x.at[:, :, pl.ds(LANES, cols)], x_sem)
    load.start()
    fetches = [
        pltpu.make_async_copy(src, dst, given_sem.at[i])
        for i, (src, dst) in enumerate(zip(given, (centers, widths, weights, colors, light)))
    ]
    for fetch in fetches:
        fetch.start()

    barrier = pltpu.get_barrier_semaphore()

    def greet(gx, gy):
        pl.semaphore_signal(barrier, inc=1, device_id=(gx, gy), device_id_type=MESH)

    greet(nxt, my)
    greet(prv, my)
    greet(me, down)
    greet(me, up)

    def greet_z(k, _):
        greet(lax.rem(z + k, nz) * Q + y, my)
        return 0

    lax.fori_loop(1, nz, greet_z, 0)
    for off in (0, per, nz - per):
        for k in range(1, Q):
            for g in range(per):
                greet(lax.rem(first_z + off + g, nz) * Q + lax.rem(y + k, Q), my)
    x[:, :, :LANES] = jnp.zeros((layers, rows, LANES), jnp.float32)
    x[:, :, LANES + cols :] = jnp.zeros((layers, rows, LANES), jnp.float32)

    def part_at(s, place):
        away = jnp.where(lax.rem(s, 2) == 0, s // 2, PARTS - (s + 1) // 2)
        return lax.rem(place // per + PARTS // 2 + away, PARTS)

    def rows_copy(side):
        return pltpu.make_async_remote_copy(
            src_ref=rows_out.at[1 - side],
            dst_ref=rows_in.at[side],
            send_sem=rows_ss.at[side],
            recv_sem=rows_rs.at[side],
            device_id=(me, down if side == 0 else up),
            device_id_type=MESH,
        )

    def depth_copy(side, s, place, gx):
        start = pl.multiple_of(part_at(s, place) * width, width)
        return pltpu.make_async_remote_copy(
            src_ref=density.at[layers - 1 if side == 0 else 0, :, pl.ds(start, width)],
            dst_ref=depth_in.at[side, :, pl.ds(start, width)],
            send_sem=depth_ss.at[side, s],
            recv_sem=depth_rs.at[side, s],
            device_id=(gx, my),
            device_id_type=MESH,
        )

    def p1_copy(s, k):
        to = lax.rem(y + k, Q)
        return pltpu.make_async_remote_copy(
            src_ref=p1s.at[s, to],
            dst_ref=p1r.at[s, k],
            send_sem=p1_ss.at[s, k],
            recv_sem=p1_rs.at[s, k],
            device_id=(z * Q + to, my),
            device_id_type=MESH,
        )

    def last_copy(s, g, k):
        at, to = lax.rem(in_group + g, per), lax.rem(y + k, Q)
        d = s - (PARTS - STRAIGHT)
        return pltpu.make_async_remote_copy(
            src_ref=p1s.at[s, to, at],
            dst_ref=lastr.at[d, g, k],
            send_sem=last_ss.at[d, g, k],
            recv_sem=last_rs.at[d, g, k],
            device_id=((part_at(s, z) * per + at) * Q + to, my),
            device_id_type=MESH,
        )

    def from_first(s):
        return lax.rem(2 * (z // per) - part_at(s, z) + 2 * PARTS, PARTS) * per

    def p2_copy(k):
        to = lax.rem(z + k, nz)
        return pltpu.make_async_remote_copy(
            src_ref=p2s.at[to],
            dst_ref=p2r.at[k],
            send_sem=p2_ss.at[k],
            recv_sem=p2_rs.at[k],
            device_id=(to * Q + y, my),
            device_id_type=MESH,
        )

    for fetch in fetches:
        fetch.wait()
    tile = (8, LANES)
    scale = math.sqrt(math.log2(math.e))
    for k in range(bumps):
        inverse = scale / jnp.full(tile, widths[k], jnp.float32)
        prm[2 * k] = jnp.full(tile, centers[k], jnp.float32)
        prm[2 * k + 1] = -inverse * inverse
    for c in range(3):
        prm[2 * bumps + c] = jnp.full(tile, 0.5 * light[c], jnp.float32)
    into = lax.broadcasted_iota(jnp.int32, (rows, DEEP), 0)
    out_of = lax.broadcasted_iota(jnp.int32, (rows, DEEP), 1)
    lines = []
    for c in range(4):
        line = jnp.zeros((rows, DEEP), jnp.float32)
        for k in range(bumps):
            factor = weights[k] * step_size if c == 0 else colors[c - 1, k] * 0.375
            line = jnp.where(out_of == into + k * rows, factor, line)
        lines.append(line)
    exact = jnp.concatenate(lines, 0)
    high = exact.astype(jnp.bfloat16)
    mix[: 4 * rows] = high
    mix[4 * rows :] = (exact - high.astype(jnp.float32)).astype(jnp.bfloat16)

    load.wait()
    for l in range(layers):
        rows_out[0, l : l + 1, :] = x[l, 0:1, LANES : LANES + cols]
        rows_out[1, l : l + 1, :] = x[l, rows - 1 : rows, LANES : LANES + cols]

    lane = lax.broadcasted_iota(jnp.int32, tile, 1)
    row = lax.broadcasted_iota(jnp.int32, tile, 0)
    lane_all = lax.broadcasted_iota(jnp.int32, (rows, LANES), 1)
    from_prv = jnp.where(me > 0, 1.0, 0.0).astype(jnp.float32)
    from_nxt = jnp.where(me < nx - 1, 1.0, 0.0).astype(jnp.float32)
    from_up = jnp.where(my > 0, 1.0, 0.0).astype(jnp.float32)
    from_down = jnp.where(my < ny - 1, 1.0, 0.0).astype(jnp.float32)
    n_row = rows // 8

    def wide(i):
        return jnp.concatenate([prm[i]] * n_row, 0)

    def split(v):
        return [v[8 * r : 8 * r + 8] for r in range(n_row)]

    def column_of(s, i):
        return pl.multiple_of(part_at(s, z) * width + i * LANES, LANES)

    def broad(i):
        return jnp.concatenate([wide(i)] * per, 1)

    def emit_layer(s, l):
        cells = x[l, :, pl.ds(pl.multiple_of(part_at(s, z) * width + LANES, LANES), width)]
        stack = []
        for k in range(bumps):
            away = cells - broad(2 * k)
            stack.append(jnp.exp2(away * away * broad(2 * k + 1)))
        if DEEP > bumps * rows:
            stack.append(jnp.zeros((DEEP - bumps * rows, width), jnp.float32))
        exact = jnp.concatenate(stack, 0)
        high = exact.astype(jnp.bfloat16)
        low = (exact - high.astype(jnp.float32)).astype(jnp.bfloat16)
        most = jnp.dot(mix[...], high, preferred_element_type=jnp.float32)
        rest = jnp.dot(mix[: 4 * rows], low, preferred_element_type=jnp.float32)
        sums = most[: 4 * rows] + (most[4 * rows :] + rest)
        t = sums[:rows]
        opacity = t * (1.0 - t * (0.5 - t * (1.0 / 6.0 - t * (1.0 / 24.0))))
        emi[s, l, 0] = opacity
        for c in range(1, 4):
            emi[s, l, c] = sums[c * rows : (c + 1) * rows]

    def march_layer(s, i, at, l, state):
        clear, opaque, colour = state
        here = pl.ds(at, LANES)

        def layer(n):
            return x[n, :, pl.ds(pl.multiple_of(at + LANES, LANES), LANES)]

        before = layer(l - 1) if l > 0 else depth_in[0, :, here] * from_prv
        after = layer(l + 1) if l < layers - 1 else depth_in[1, :, here] * from_nxt
        tiles = split(layer(l))
        left = split(x[l, :, pl.ds(at, LANES)])
        right = split(x[l, :, pl.ds(pl.multiple_of(at + 2 * LANES, LANES), LANES)])
        over_row = jnp.broadcast_to(rows_in[0, l : l + 1, here], tile) * from_up
        under_row = jnp.broadcast_to(rows_in[1, l : l + 1, here], tile) * from_down
        behind = [shifted([t], 1, e, lane, 1)[0] for t, e in zip(tiles, left)]
        ahead = [shifted([t], -1, e, lane, 1)[0] for t, e in zip(tiles, right)]
        above = shifted(tiles, 1, over_row, row, 0)
        below = shifted(tiles, -1, under_row, row, 0)
        hx, hy, hz = (wide(2 * bumps + c) for c in range(3))
        facing = (
            hx * (after - before)
            + hy * jnp.concatenate([b - a for a, b in zip(above, below)], 0)
            + hz * jnp.concatenate([b - a for a, b in zip(behind, ahead)], 0)
        )
        shading = 5.0 / 3.0 + jnp.tanh(facing)
        local = pl.ds(pl.multiple_of(i * LANES, LANES), LANES)
        seen = clear * emi[s, l, 0, :, local]
        lit = seen * shading
        return clear - seen, opaque + seen, [colour[c] + lit * emi[s, l, c + 1, :, local] for c in range(3)]

    def march_end(s, i, state):
        owned = regroup(state[2] + [state[1]], lane_all)
        for j in range(Q):
            p1s[s, j, i] = owned[j]

    zero = jnp.zeros((rows, LANES), jnp.float32)
    fresh = (jnp.ones((rows, LANES), jnp.float32), zero, [zero] * 3)

    def emit(s):
        def one(n, _):
            for l in range(layers // per):
                emit_layer(s, n * (layers // per) + l)
            return 0

        lax.fori_loop(0, per, one, 0)

    def march(s):
        def one(i, _):
            at, state = column_of(s, i), fresh
            for l in range(layers):
                state = march_layer(s, i, at, l, state)
            march_end(s, i, state)
            return 0

        lax.fori_loop(0, per, one, 0)

    def emit_and_march(e, s):
        def one(i, _):
            at, state = column_of(s, i), fresh
            for l in range(layers):
                if l % per == 0:
                    emit_layer(e, i * (layers // per) + l // per)
                state = march_layer(s, i, at, l, state)
            march_end(s, i, state)
            return 0

        lax.fori_loop(0, per, one, 0)

    emit(0)
    pl.semaphore_wait(barrier, 4 + (nz - 1) + 3 * per * (Q - 1))

    def send_depth(s):
        depth_copy(0, s, nxt // Q, nxt).start()
        depth_copy(1, s, prv // Q, prv).start()

    send_depth(0)
    for side in range(2):
        rows_copy(side).start()
    for s in range(1, LEAD):
        send_depth(s)
    for s in range(1, LEAD):
        emit(s)

    def send_more(s, _):
        send_depth(s)
        return 0

    lax.fori_loop(LEAD, PARTS, send_more, 0)
    for side in range(2):
        rows_copy(side).wait_recv()


    def step(s, _):
        @pl.when(s < PARTS)
        def _():
            for side in range(2):
                depth_copy(side, s, z, (nxt, prv)[side]).wait_recv()

        @pl.when(s + LEAD < PARTS)
        def _():
            emit_and_march(s + LEAD, s)

        @pl.when((s + LEAD >= PARTS) & (s < PARTS))
        def _():
            march(s)

        @pl.when(s < PARTS - STRAIGHT)
        def _():
            for k in (2, 1, 3):
                p1_copy(s, k).start()

        @pl.when(s >= PARTS - STRAIGHT)
        def _():
            @pl.when(s < PARTS - 1)
            def _():
                last_copy(s, 0, 0).start()

            for g in range(per):
                for k in range(Q):
                    if (g, k) != (0, 0):
                        last_copy(s, g, k).start()

        @pl.when((s >= 2) & (s < PARTS - STRAIGHT + 2))
        def _():
            t = s - 2
            first = part_at(t, z) * per
            p1r[t, 0] = p1s[t, y]
            for k in range(1, Q):
                p1_copy(t, k).wait_recv()
            flat = (per * rows, LANES)
            lane_flat = lax.broadcasted_iota(jnp.int32, flat, 1)
            total = p1r[t, lax.rem(y + 1, Q)].reshape(flat)
            for j in range(Q - 2, -1, -1):
                total = over(p1r[t, lax.rem(y + Q - j, Q)].reshape(flat), total, lane_flat)
            total = total.reshape(per, rows, LANES)
            for b in range(per):
                p2s[first + b] = total[b]
                p2_copy(lax.rem(first + b + nz - z, nz)).start()

        return 0

    lax.fori_loop(0, PARTS, step, 0)

    for side in range(2):
        rows_copy(side).wait_send()

    def finish(s, _):
        for side in range(2):
            depth_copy(side, s, z, (nxt, prv)[side]).wait_send()

        @pl.when(s < PARTS - STRAIGHT)
        def _():
            for k in range(1, Q):
                p1_copy(s, k).wait_send()

        return 0

    lax.fori_loop(0, PARTS, finish, 0)

    lastr[STRAIGHT - 1, 0, 0] = p1s[PARTS - 1, y, in_group]

    def join_last(d, _):
        s = d + PARTS - STRAIGHT

        @pl.when(s < PARTS - 1)
        def _():
            last_copy(s, 0, 0).wait()

        for g in range(per):
            for k in range(Q):
                if (g, k) != (0, 0):
                    last_copy(s, g, k).wait()
        for g in range(per):
            near = lax.rem(in_group + per - g, per)
            total = lastr[d, near, lax.rem(y + 1, Q)]
            for j in range(Q - 2, -1, -1):
                total = over(lastr[d, near, lax.rem(y + Q - j, Q)], total, lane_all)
            p2r[lax.rem(z + nz - (from_first(s) + g), nz)] = total
        return 0

    lax.fori_loop(0, STRAIGHT, join_last, 0)

    def finish_p2(s, _):
        for g in range(per):
            p2_copy(lax.rem(part_at(s, z) * per + g + nz - z, nz)).wait_send()
            p2_copy(lax.rem(z + nz - (from_first(s) + g), nz)).wait_recv()
        return 0

    lax.fori_loop(0, PARTS - STRAIGHT, finish_p2, 0)

    total = p2r[lax.rem(z + 1, nz)]
    for i in range(1, nz):
        total = over(p2r[lax.rem(z + 1 + i, nz)], total, lane_all)
    for c in range(4):
        out[c] = total[:, G * c : G * c + G]


def local(nx, ny, density, centers, widths, weights, colors, light):
    layers, rows, cols = density.shape
    nz, bumps = nx // Q, centers.shape[0]
    width = cols // PARTS
    per = width // LANES
    dma = pltpu.SemaphoreType.DMA
    hbm = pl.BlockSpec(memory_space=pltpu.HBM)
    f32 = jnp.float32
    return pl.pallas_call(
        functools.partial(kernel, nx, ny, 1.5 / (layers * nx)),
        out_shape=jax.ShapeDtypeStruct((4, rows, cols // nx), f32),
        in_specs=[hbm] * 6,
        out_specs=pl.BlockSpec(memory_space=pltpu.VMEM),
        scratch_shapes=[pltpu.SMEM(given.shape, f32) for given in (centers, widths, weights, colors, light)]
        + [
            pltpu.VMEM((layers, rows, cols + 2 * LANES), f32),
            pltpu.VMEM((2, layers, cols), f32),
            pltpu.VMEM((2, layers, cols), f32),
            pltpu.VMEM((2, rows, cols), f32),
            pltpu.VMEM((2 * bumps + 3, 8, LANES), f32),
            pltpu.VMEM((8 * rows, DEEP), jnp.bfloat16),
            pltpu.VMEM((PARTS, layers, 4, rows, width), f32),
            pltpu.VMEM((PARTS, Q, per, rows, LANES), f32),
            pltpu.VMEM((PARTS - 1, Q, per, rows, LANES), f32),
            pltpu.VMEM((STRAIGHT, per, Q, rows, LANES), f32),
            pltpu.VMEM((nz, rows, LANES), f32),
            pltpu.VMEM((nz, rows, LANES), f32),
            dma,
            dma((5,)),
            dma((2,)),
            dma((2,)),
            dma((2, PARTS)),
            dma((2, PARTS)),
            dma((PARTS - 1, Q)),
            dma((PARTS - 1, Q)),
            dma((STRAIGHT, per, Q)),
            dma((STRAIGHT, per, Q)),
            dma((nz,)),
            dma((nz,)),
        ],
        compiler_params=pltpu.CompilerParams(
            collective_id=0, has_side_effects=True, vmem_limit_bytes=40 * 1024 * 1024
        ),
        cost_estimate=pl.CostEstimate(
            flops=130 * density.size, bytes_accessed=4 * density.size, transcendentals=9 * density.size
        ),
    )(*(pltpu.with_memory_space_constraint(v, pltpu.HBM) for v in (density, centers, widths, weights, colors, light)))


def solution(mesh):
    nx, ny = mesh.shape["gx"], mesh.shape["gy"]
    in_specs = (P("gx", "gy", None), P(), P(), P(), P(), P())
    out_specs = P(None, "gy", "gx")
    return jax.shard_map(
        functools.partial(local, nx, ny), mesh=mesh, in_specs=in_specs, out_specs=out_specs, check_vma=False
    )
```
